32 devices in a mesh: lat: 2 (over x), dp: 8 (over z, core), exp: 2 (over y).
Axes of the slice: x: 2, y: 2, z: 4, core: 2. Of those that a mesh axis runs over, the one named last changes fastest.
Arguments:
- images: bfloat16 [16, 32, 256, 192], P(('dp', 'exp'), 'lat'), may hold values from -6 to 6
- cotangent: bfloat16 [16, 32, 256, 192], P(('dp', 'exp'), 'lat'), may hold values from -0.15625 to 0.15625
- labels: int32 [16, 32, 2, 1], P(('dp', 'exp'), 'lat'), may hold values from 0 to 15; in each aligned block of 32 rows (0 to 31, 32 to 63, ..., all dimensions but the last counted through in order) at most 3 rows name the same one
- dw_kernel: float32 [7, 7, 192], replicated, may hold values from -0.875 to 0.875
- ln_gain: float32 [192], replicated, may hold values from 0.5 to 2
- w_expand: bfloat16 [192, 768], replicated, may hold values from -0.4375 to 0.4375
- w_reduce: bfloat16 [768, 192], replicated, may hold values from -0.21875 to 0.21875
- exp_in: bfloat16 [16, 192, 768], P('exp'), may hold values from -0.4375 to 0.4375
- exp_out: bfloat16 [16, 768, 192], P('exp'), may hold values from -0.21875 to 0.21875
Outputs:
- output: bfloat16 [16, 32, 256, 192], P(('dp', 'exp'), 'lat')
- grad_in: float32 [16, 192, 768], P('exp')
- grad_out: float32 [16, 768, 192], P('exp')
The draws below stay inside these ranges and needn't reach their ends.
Inputs may be any that keep to these rules, and one draw needn't show every extreme that they name: `labels`: among the 32 row blocks of one device (aligned runs of 32 blocks in the order clip, row, block), no class is named more than 3 times, a bound that some block reaches.
All inputs are finite; a program needn't handle non-finite values.
Results may differ from the reference program's by a relative error of at most 0.0072.
Values may be sent and summed in bfloat16 or wider, within the bound.
No kernel may reach another device: no remote copies, remote signals or barrier semaphores. Data moves between devices by JAX's collectives and lax.ppermute only.
A program may use at most 128 MiB of HBM per device.

```python
import math
import jax
import jax.numpy as jnp
import numpy as np
from jax import lax

C = 192
FF = 768
EXPERTS = 16
W = 256
BLOCK = 128
H = 32
CLIPS = 16
NB = 2
BLK_DEV = 32
CAP = 3
DEVICES = 32


def shard_levels(own_key, dims, shards, low, high):
    def one(position, parts):
        draws = jax.random.uniform(jax.random.fold_in(jax.random.fold_in(own_key, 6), position), (parts,), jnp.float32, low / len(shards), high / len(shards))
        return jnp.repeat(jnp.exp(draws), dims[position] // parts).reshape((-1,) + (1,) * (len(dims) - position - 1))

    level = one(*shards[0])
    for cut in shards[1:]:
        level = level * one(*cut)
    return level


def assign_block(key, own, number, rows, number_of, top, most, skew):
    order = jax.random.permutation(key, number_of)
    packed, ordinary = load_shares(number_of, rows * top, most, skew, True), load_shares(number_of, rows * top, most, skew, False)
    places = jnp.arange(number_of)

    def named(tallies, rotation):
        used = int((tallies > 0).sum())
        fixed = max(1, used // 4)
        shifted = fixed + (places - fixed + rotation * (used - fixed)) % max(1, number_of - fixed)
        return jnp.zeros((number_of,), jnp.int32).at[order[jnp.where(places < fixed, places, shifted)]].set(jnp.asarray(tallies, jnp.int32))

    tallies = jnp.where(number % 4 == 0, named(packed, number // 4), named(ordinary, number - number // 4 - 1))
    mixed = jax.random.permutation(jax.random.fold_in(own, 3), number_of)
    donor, sink = mixed[0:number_of // 2 * 2:2], mixed[1:number_of // 2 * 2:2]
    margin = jnp.minimum(tallies[donor] - 1, most - tallies[sink]) // 2
    margin = jnp.where((donor == order[0]) | (sink == order[0]) | (tallies[sink] == 0), 0, jnp.maximum(margin, 0))
    shifted = jax.random.randint(jax.random.fold_in(own, 4), (number_of // 2,), 0, 1 << 20) % (margin + 1)
    tallies = tallies.at[donor].add(-shifted).at[sink].add(shifted)
    items = jnp.searchsorted(jnp.cumsum(tallies), jnp.arange(rows * top), side="right").astype(jnp.int32)
    table = items.reshape(top, rows).T
    table = table[jax.random.permutation(jax.random.fold_in(own, 1), rows)]
    rotation = jax.random.randint(jax.random.fold_in(own, 2), (rows, 1), 0, top)
    return jnp.take_along_axis(table, (jnp.arange(top)[None, :] + rotation) % top, axis=1)


def load_shares(amount, total, most, skew, full):
    portions = [(1 << 20) // math.isqrt(grade ** skew) + 1 for grade in range(1, amount + 1)]
    largest = most if full else min(most, max(-(-total // amount), total * portions[0] // sum(portions)))
    least = 1 if total - largest >= amount - 1 else 0
    given, surplus = [largest] + [least] * (amount - 1), total - largest - least * (amount - 1)
    while surplus > 0:
        candidates = [i for i in range(1, amount) if given[i] < largest] or [i for i in range(1, amount) if given[i] < most]
        pool, remaining = sum([portions[i] for i in candidates]), surplus
        for i in candidates:
            addition = min(most - given[i], max(1, remaining * portions[i] // pool), surplus)
            given[i] = given[i] + addition
            surplus = surplus - addition
    return np.array(given)


def normal_values(stream_key, extent, scale, reach, shards=(), kind=jnp.bfloat16):
    factor_of = shard_levels(stream_key, extent, shards, -0.22, 0.18) if shards else 1.0
    array = jax.random.normal(stream_key, extent, jnp.float32) * scale * factor_of
    return jnp.minimum(jnp.maximum(array, -reach), reach).astype(kind)


def setup_inputs(seed: int = 0) -> dict:
    streams_of = jax.random.split(jax.random.key(seed), 10)
    images = normal_values(streams_of[0], (CLIPS, H, W, C), 1.0, 6.0, ((0, 16), (1, 2)))
    cotangent = normal_values(streams_of[1], (CLIPS, H, W, C), ((EXPERTS / (CLIPS * H * W)) ** 0.5), 0.15625, ((0, 16), (1, 2)))
    labels_keys = jax.random.split(jax.random.fold_in(streams_of[2], 1), CLIPS * H * NB // BLK_DEV)
    labels_turns = jax.random.permutation(jax.random.fold_in(streams_of[2], 3), CLIPS * H * NB // BLK_DEV)
    labels = jax.vmap(lambda own, number: assign_block(jax.random.fold_in(streams_of[2], 2), own, number, BLK_DEV, EXPERTS, 1, CAP, 2))(labels_keys, labels_turns).reshape((CLIPS, H, NB, 1))
    dw_kernel = normal_values(streams_of[3], (7, 7, C), 49 ** -0.5, 0.875, (), jnp.float32)
    ln_gain = jnp.clip(jnp.exp(jax.random.uniform(streams_of[4], (C,), jnp.float32, math.log(0.5), math.log(2.0))), 0.5, 2.0)
    w_expand = normal_values(streams_of[5], (C, FF), C ** -0.5, 0.4375)
    w_reduce = normal_values(streams_of[6], (FF, C), FF ** -0.5, 0.21875)
    exp_in = normal_values(streams_of[7], (EXPERTS, C, FF), C ** -0.5, 0.4375, ((0, 2),))
    exp_out = normal_values(streams_of[8], (EXPERTS, FF, C), FF ** -0.5, 0.21875, ((0, 2),))
    return {"images": images, "cotangent": cotangent, "labels": labels, "dw_kernel": dw_kernel, "ln_gain": ln_gain, "w_expand": w_expand, "w_reduce": w_reduce, "exp_in": exp_in, "exp_out": exp_out}


def gelu_slope(values):
    return 0.5 * (1.0 + lax.erf(values * 0.7071067811865476)) + values * jnp.exp(-0.5 * values * values) * 0.3989422804014327

def depthwise(padded, kernel):
    row_count = padded.shape[1] - 6
    col_count = padded.shape[2] - 6
    summed = jnp.zeros((padded.shape[0], row_count, col_count, padded.shape[3]), jnp.float32)
    for row_off in range(7):
        for col_off in range(7):
            window = padded[:, row_off:row_off + row_count, col_off:col_off + col_count, :]
            summed = summed + window.astype(jnp.float32) * kernel[row_off, col_off]
    return summed

def dense_block(images, smoothed, ln_gain, w_expand, w_reduce):
    channels = images.shape[-1]
    channel_mean = lax.optimization_barrier(jnp.mean(smoothed, axis=-1, keepdims=True))
    centered = smoothed - channel_mean
    variance = lax.optimization_barrier(jnp.mean(centered * centered, axis=-1, keepdims=True))
    normed = (centered * lax.rsqrt(variance + 1e-06) * ln_gain).astype(jnp.bfloat16)
    flat_normed = normed.reshape(-1, channels)
    expanded = jnp.dot(flat_normed, w_expand, preferred_element_type=jnp.float32)
    active = jax.nn.gelu(expanded, approximate=False).astype(jnp.bfloat16)
    reduced = jnp.dot(active, w_reduce, preferred_element_type=jnp.float32)
    dense_out = images.reshape(-1, channels).astype(jnp.float32) + reduced
    return dense_out.astype(jnp.bfloat16).reshape(images.shape)

def expert_pass(inputs, grads_in, w_in, w_out):
    pre_act = jnp.dot(inputs, w_in, preferred_element_type=jnp.float32)
    hidden = jax.nn.gelu(pre_act, approximate=False).astype(jnp.bfloat16)
    outputs = jnp.dot(hidden, w_out, preferred_element_type=jnp.float32).astype(jnp.bfloat16)
    grad_out = jnp.dot(hidden.T, grads_in, preferred_element_type=jnp.float32)
    back_prop = jnp.dot(grads_in, w_out.T, preferred_element_type=jnp.float32)
    scaled = (back_prop * gelu_slope(pre_act)).astype(jnp.bfloat16)
    grad_in = jnp.dot(inputs.T, scaled, preferred_element_type=jnp.float32)
    return (outputs, grad_in, grad_out)

def reference(images, cotangent, labels, dw_kernel, ln_gain, w_expand, w_reduce, exp_in, exp_out):
    channels = images.shape[-1]

    def one_image(picture):
        padded = jnp.pad(picture[None], ((0, 0), (3, 3), (3, 3), (0, 0)))
        return dense_block(picture[None], depthwise(padded, dw_kernel), ln_gain, w_expand, w_reduce)[0]
    dense_out = lax.map(one_image, images)
    blocks = dense_out.reshape(-1, BLOCK * channels)
    grad_blocks = cotangent.reshape(-1, BLOCK * channels)
    flat_labels = labels.reshape(-1).astype(jnp.int32)
    most_blocks = DEVICES * CAP

    def per_expert(gathered_out, expert):
        member = flat_labels == expert
        chosen = jnp.nonzero(member, size=most_blocks, fill_value=0)[0].astype(jnp.int32)
        live_count = jnp.sum(member.astype(jnp.int32))
        is_live = (jnp.arange(most_blocks, dtype=jnp.int32) < live_count)[:, None]
        inputs = blocks[chosen].reshape(-1, channels)
        grads_in = jnp.where(is_live, grad_blocks[chosen], jnp.zeros((), jnp.bfloat16)).reshape(-1, channels)
        outputs, grad_in, grad_out = expert_pass(inputs, grads_in, exp_in[expert], exp_out[expert])
        outputs = jnp.where(is_live, outputs.reshape(most_blocks, -1), jnp.zeros((), jnp.bfloat16))
        gathered_out = gathered_out.at[chosen].add(outputs)
        return (gathered_out, (grad_in, grad_out))
    empty_out = jnp.zeros(blocks.shape, jnp.bfloat16)
    expert_out, grads = lax.scan(per_expert, empty_out, jnp.arange(EXPERTS, dtype=jnp.int32))
    output = (dense_out.astype(jnp.float32) + expert_out.reshape(dense_out.shape).astype(jnp.float32)).astype(jnp.bfloat16)
    return (output, grads[0], grads[1])
```

```python
import functools
import jax
import jax.numpy as jnp
import numpy as np
from jax import lax
from jax.experimental import pallas as pl
from jax.experimental.pallas import tpu as pltpu
from jax.sharding import PartitionSpec as P

EXPERTS = 16
BLOCK = 128
CAP = 3
SEG = 8
TILE = 4
SIZES = (4, 4)
BF = jnp.bfloat16
F32 = jnp.float32
VMEM_LIMIT = 56 << 20
ANY = pl.BlockSpec(memory_space=pl.ANY)
VM = pl.BlockSpec(memory_space=pltpu.VMEM)
SM = pl.BlockSpec(memory_space=pltpu.SMEM)


def params(**more):
    return pltpu.CompilerParams(vmem_limit_bytes=VMEM_LIMIT, **more)


def cost(flops):
    return pl.CostEstimate(flops=flops, transcendentals=0, bytes_accessed=1 << 20)


def dot(a, b, dims=((1,), (0,))):
    return lax.dot_general(a, b, (dims, ((), ())), preferred_element_type=F32)


def dense_kernel(place, table, counts, images, halo, dw, gain, w1, w2, spread, gather, sums, *refs):
    dense, slots, (wide, smooth, taps, gains, w1s) = refs[0], refs[1:-5], refs[-5:]
    rows, channels, width = images.shape
    steps = width // SEG
    rest = channels - 128
    step = pl.program_id(0)
    first = step * TILE

    @pl.when(step == 0)
    def _():
        for i in range(7):
            row = dw[i]
            low, high = row[:, :128], row[:, 128:]
            for n, pair in ((0, [low, high, high]), (49, [low, low])):
                joined = jnp.concatenate(pair, axis=1)
                for j in range(7):
                    one = jnp.broadcast_to(joined[j : j + 1], (SEG, 256))
                    taps[n + 7 * i + j] = one.astype(BF)
        zero = jnp.zeros((1, rest), F32)
        low, high = gain[:, :128], gain[:, 128:]
        gains[0] = jnp.concatenate([low, high, zero], axis=1)
        gains[1] = jnp.concatenate([low, zero, high], axis=1)
        zero = jnp.zeros((rest, w1.shape[1]), BF)
        w1s[0, :128] = w1[:128]
        w1s[0, 128 : 128 + rest] = w1[128:]
        w1s[0, 128 + rest :] = zero
        w1s[1, :128] = w1[:128]
        w1s[1, 128 : 256 - rest] = zero
        w1s[1, 256 - rest :] = w1[128:]

    def picture_row(q):
        g = first - 3 + q
        inside = jnp.logical_and(g >= 0, g < rows)
        row = images[jnp.clip(g, 0, rows - 1)]
        wanted = jnp.where(place[3] == 0, g >= rows, g < 0)
        other = halo[jnp.clip(jnp.where(g < 0, g + 3, g - rows), 0, 2)]
        other = jnp.where(wanted, other, jnp.zeros_like(other))
        return jnp.where(inside, row, other)

    picture = [picture_row(q) for q in range(TILE + 6)]
    tall = []
    for q in range(TILE + 6):
        partner = picture[min(q + 2, TILE + 5)]
        joined = jnp.concatenate([picture[q], partner[128:]], axis=0)
        tall.append(dot(spread[...], joined, ((1,), (1,))))
    for q in range(TILE + 4):
        wide[q] = tall[q].astype(BF).reshape(steps + 6, SEG, 256)
    for q in range(7):
        joined = jnp.concatenate([tall[q + 2][:, :128], tall[q + 3][:, :128]], axis=1)
        wide[TILE + 4 + q] = joined.astype(BF).reshape(steps + 6, SEG, 256)

    part = 8
    parts = steps // part

    def conv(n, carry):
        unit, start = n // parts, n % parts * part
        row = jnp.where(unit == 2, TILE + 4, unit)
        kind = jnp.where(unit == 2, 49, 0)
        total = jnp.zeros((part, SEG, 256), F32)
        for i in range(7):
            source = wide[row + i, pl.ds(start, part + 6)]
            terms = [source[j : j + part] * taps[kind + 7 * i + j][None] for j in range(7)]
            low = (terms[0] + terms[1]) + (terms[2] + terms[3])
            high = (terms[4] + terms[5]) + terms[6]
            total = total + (low + high).astype(F32)
        smooth[unit, pl.ds(start, part)] = total.astype(BF)
        return carry

    lax.fori_loop(0, 3 * parts, conv, 0)

    units = [smooth[u].reshape(width, 256) for u in range(3)]
    both = [
        units[0],
        units[1],
        jnp.concatenate([units[2][:, :128], units[0][:, 128:]], axis=1),
        jnp.concatenate([units[2][:, 128:], units[1][:, 128:]], axis=1),
    ]
    every = range(TILE)
    values = [dot(gather[...], both[h]) for h in every]
    mean = [dot(values[h].astype(BF), sums[h // 2]) * (1.0 / channels) for h in every]
    c0 = [values[h][:, :128] - mean[h] for h in every]
    c1 = [values[h][:, 128:] - mean[h] for h in every]
    squares = [
        jnp.concatenate([(c0[h] * c0[h]).astype(BF), (c1[h] * c1[h]).astype(BF)], axis=1)
        for h in every
    ]
    scale = [
        lax.rsqrt(dot(squares[h], sums[h // 2]) * (1.0 / channels) + 1e-6) for h in every
    ]
    normed = [
        jnp.concatenate(
            [
                (c0[h] * scale[h] * gains[h // 2][:, :128]).astype(BF),
                (c1[h] * scale[h] * gains[h // 2][:, 128:]).astype(BF),
            ],
            axis=1,
        )
        for h in every
    ]
    active = []
    for h in every:
        expanded = dot(normed[h], w1s[h // 2])
        halved = 0.5 * expanded
        active.append((halved + halved * lax.erf(expanded * 0.7071067811865476)).astype(BF))
    for h in every:
        result = images[first + h].astype(F32) + dot(w2[...], active[h], ((1,), (1,)))
        dense[first + h] = result.astype(BF)

    @pl.when(step == pl.num_programs(0) - 1)
    def _():
        copy_slots(place, table, dense, slots)


def dense_constants(width, channels):
    steps = width // SEG
    spread = np.zeros((steps + 6, SEG, width), np.float32)
    gather = np.zeros((width, steps, SEG), np.float32)
    for s in range(SEG):
        for t in range(steps + 6):
            if 0 <= s * steps + t - 3 < width:
                spread[t, s, s * steps + t - 3] = 1
        for t in range(steps):
            gather[s * steps + t, t, s] = 1
    rest = channels - 128
    sums = np.zeros((2, 256, 128), np.float32)
    sums[:, :128] = 1
    sums[0, 128 : 128 + rest] = 1
    sums[1, 256 - rest :] = 1
    return (
        jnp.asarray(spread.reshape(-1, width), BF),
        jnp.asarray(gather.reshape(width, width), BF),
        jnp.asarray(sums, BF),
    )


def slot_shapes(channels):
    return [jax.ShapeDtypeStruct((CAP * size, channels, BLOCK), BF) for size in SIZES]


def dense_part(images, halo, dw_kernel, ln_gain, w_expand, w_reduce, place, table, counts):
    rows, channels, width = images.shape
    steps = width // SEG
    hidden = w_expand.shape[1]
    args = [images, halo, dw_kernel, ln_gain[None], w_expand, w_reduce]
    args += dense_constants(width, channels)
    slots = slot_shapes(channels)
    return pl.pallas_call(
        dense_kernel,
        grid=(rows // TILE,),
        in_specs=[SM] * 3 + [VM] * len(args),
        out_specs=[VM] * (1 + len(slots)),
        out_shape=[jax.ShapeDtypeStruct(images.shape, BF)] + slots,
        scratch_shapes=[
            pltpu.VMEM((TILE + 11, steps + 6, SEG, 256), BF),
            pltpu.VMEM((3, steps, SEG, 256), BF),
            pltpu.VMEM((98, SEG, 256), BF),
            pltpu.VMEM((2, 1, 256), F32),
            pltpu.VMEM((2, 256, hidden), BF),
        ],
        compiler_params=params(),
        cost_estimate=cost(64 << 30),
        name="dense_block",
    )(place, table, counts, *args)


def at_block(ref, b):
    return ref.at[b // 2, :, pl.ds(pl.multiple_of(b % 2 * BLOCK, BLOCK), BLOCK)]


def block_of(ref, b):
    return ref[b // 2, :, pl.ds(pl.multiple_of(b % 2 * BLOCK, BLOCK), BLOCK)]


def copy_slots(place, table, blocks, slots):
    n = CAP * place[1]
    for slot in slots:
        for k in range(slot.shape[0]):
            slot[k] = block_of(blocks, table[n + k])
        n = n + slot.shape[0]


def route_kernel(labels, place, blocks, *refs):
    table, counts, slots = refs[0], refs[1], refs[2:]
    for e in range(EXPERTS):
        counts[e] = 0
        for k in range(CAP):
            table[CAP * e + k] = 0

    def step(b, carry):
        e = labels[b]
        k = counts[e]
        table[CAP * e + k] = b
        counts[e] = k + 1
        return carry

    lax.fori_loop(0, labels.shape[0], step, 0)
    copy_slots(place, table, blocks, slots)


def route(blocks, labels, place):
    slots = slot_shapes(blocks.shape[1])
    return pl.pallas_call(
        route_kernel,
        in_specs=[SM, SM, VM],
        out_specs=[SM, SM] + [VM] * len(slots),
        out_shape=[
            jax.ShapeDtypeStruct((CAP * EXPERTS,), jnp.int32),
            jax.ShapeDtypeStruct((EXPERTS,), jnp.int32),
        ]
        + slots,
        compiler_params=params(),
        name="route_blocks",
    )(labels, place, blocks)


def expert_kernel(
    offset, tables, tallies, theirs, place, dense_in, cots, xs, gs, w_in, w_out,
    dense, back, keep, send, xbuf, gbuf, obuf, acc, w_in_t, w_out_t, sems,
):
    base = place[0] + offset
    group = w_in.shape[0]
    core, lat = place[2], place[3]
    counts = [tallies[base + k] for k in range(group)]
    counts2 = [theirs[base + k] for k in range(group)]
    table = [tables[CAP * base + n] for n in range(CAP * group)]

    def spot_of(k, j):
        return pl.ds(pl.multiple_of((counts[k] + j) * BLOCK, BLOCK), BLOCK)

    def own_copies(k, j):
        b, here = table[CAP * k + j], pl.ds(j * BLOCK, BLOCK)
        return (
            pltpu.make_async_copy(at_block(dense_in, b), xbuf.at[k, :, here], sems.at[0, k, j]),
            pltpu.make_async_copy(at_block(cots, b), gbuf.at[k, :, here], sems.at[1, k, j]),
        )

    def far_copies(k, j):
        here = spot_of(k, j)
        return (
            pltpu.make_async_copy(xs.at[CAP * k + j], xbuf.at[k, :, here], sems.at[2, k, j]),
            pltpu.make_async_copy(gs.at[CAP * k + j], gbuf.at[k, :, here], sems.at[3, k, j]),
        )

    def own_back(k, j):
        here = pl.ds(j * BLOCK, BLOCK)
        there = at_block(dense, table[CAP * k + j])
        return (pltpu.make_async_copy(xbuf.at[k, :, here], there, sems.at[0, k, j]),)

    def far_back(k, j):
        here = spot_of(k, j)
        return (pltpu.make_async_copy(obuf.at[k, :, here], back.at[CAP * k + j], sems.at[2, k, j]),)

    def each(k, tally, copies, action):
        for j in range(CAP):
            @pl.when(j < tally[k])
            def _():
                for copy in copies(k, j):
                    action(copy)

    def start(copy):
        copy.start()

    def wait(copy):
        copy.wait()

    for k in range(group):
        each(k, counts, own_copies, start)
        each(k, counts2, far_copies, start)
        total = counts[k] + counts2[k]
        for j in range(2 * CAP):
            @pl.when(jnp.logical_and(j >= total, jnp.logical_or(j < 4, total > 4)))
            def _():
                here = pl.ds(j * BLOCK, BLOCK)
                zero = jnp.zeros((xbuf.shape[1], BLOCK), BF)
                xbuf[k, :, here] = zero
                gbuf[k, :, here] = zero

    for k in range(group):
        w_in_t[...] = w_in[k].T
        w_out_t[...] = w_out[k].T
        each(k, counts, own_copies, wait)
        each(k, counts2, far_copies, wait)

        def tokens(first, many):
            here = pl.ds(first * BLOCK, many * BLOCK)
            x, g = xbuf[k, :, here], gbuf[k, :, here]
            pre = dot(w_in_t[...], x)
            share = 0.5 + 0.5 * lax.erf(pre * 0.7071067811865476)
            hidden = (pre * share).astype(BF)
            slope = share + pre * (jnp.exp(pre * pre * -0.5) * 0.3989422804014327)
            scaled = (dot(w_out_t[...], g) * slope).astype(BF)
            obuf[k, :, here] = dot(w_out[k], hidden).astype(BF)
            return dot(x, scaled, ((1,), (1,))), dot(g, hidden, ((1,), (1,)))

        acc[0], acc[1] = tokens(0, 4)

        @pl.when(counts[k] + counts2[k] > 4)
        def _():
            more = tokens(4, 2)
            acc[0] += more[0]
            acc[1] += more[1]

        spot = (k + lat * (group // 2)) % group
        grad_in, grad_out = acc[0].astype(BF), acc[1].astype(BF)
        first = core == 0
        keep[spot] = jnp.where(first, grad_in, grad_out)
        send[spot] = jnp.where(first, grad_out, grad_in)
        each(k, counts2, far_back, start)
        for j in range(CAP):
            here = pl.ds(j * BLOCK, BLOCK)

            @pl.when(j < counts[k])
            def _():
                both = xbuf[k, :, here].astype(F32) + obuf[k, :, here].astype(F32)
                xbuf[k, :, here] = both.astype(BF)

        each(k, counts, own_back, start)

    for k in range(group):
        each(k, counts2, far_back, wait)
        each(k, counts, own_back, wait)


def expert_part(offset, size, table, counts, theirs, place, dense, cots, xs, gs, exp_in, exp_out):
    channels, hidden = exp_in.shape[1:]
    tokens = 2 * CAP * BLOCK
    group = size
    weights = pl.BlockSpec((group, channels, hidden), lambda i: (offset // size, 0, 0))
    return pl.pallas_call(
        functools.partial(expert_kernel, offset),
        grid=(1,),
        in_specs=[SM, SM, SM, SM, ANY, ANY, ANY, ANY, weights, weights],
        out_specs=[ANY, ANY, VM, VM],
        out_shape=[
            jax.ShapeDtypeStruct(dense.shape, BF),
            jax.ShapeDtypeStruct(xs.shape, BF),
            jax.ShapeDtypeStruct((group, channels, hidden), BF),
            jax.ShapeDtypeStruct((group, channels, hidden), BF),
        ],
        input_output_aliases={4: 0},
        scratch_shapes=[
            pltpu.VMEM((group, channels, tokens), BF),
            pltpu.VMEM((group, channels, tokens), BF),
            pltpu.VMEM((group, channels, tokens), BF),
            pltpu.VMEM((2, channels, hidden), F32),
            pltpu.VMEM((hidden, channels), BF),
            pltpu.VMEM((hidden, channels), BF),
            pltpu.SemaphoreType.DMA((4, group, CAP)),
        ],
        compiler_params=params(),
        cost_estimate=cost(64 << 30),
        name="expert_group",
    )(table, counts, theirs, place, dense, cots, xs, gs, exp_in, exp_out)


def combine_kernel(experts, tables, tallies, place, dense_in, *refs):
    backs, (dense, xbuf, obuf, sems) = refs[:-4], refs[-4:]
    counts = [tallies[place[1] + e] for e in range(experts)]
    table = [tables[CAP * place[1] + n] for n in range(CAP * experts)]

    def each(body):
        for slot in range(CAP * experts):
            @pl.when(slot % CAP < counts[slot // CAP])
            def _():
                body(slot)

    places = [back.at[k] for back in backs for k in range(back.shape[0])]

    def fetches(slot):
        back = places[slot]
        return (
            pltpu.make_async_copy(at_block(dense_in, table[slot]), xbuf.at[slot], sems.at[0, slot]),
            pltpu.make_async_copy(back, obuf.at[slot], sems.at[1, slot]),
        )

    def store(slot):
        return pltpu.make_async_copy(xbuf.at[slot], at_block(dense, table[slot]), sems.at[0, slot])

    def begin(slot):
        for copy in fetches(slot):
            copy.start()

    def work(slot):
        for copy in fetches(slot):
            copy.wait()
        xbuf[slot] = (xbuf[slot].astype(F32) + obuf[slot].astype(F32)).astype(BF)
        store(slot).start()

    each(begin)
    each(work)
    each(lambda slot: store(slot).wait())


def combine(dense, backs, table, counts, place, experts):
    slots = CAP * experts
    channels = dense.shape[1]
    return pl.pallas_call(
        functools.partial(combine_kernel, experts),
        in_specs=[SM] * 3 + [ANY] * (1 + len(backs)),
        out_specs=ANY,
        out_shape=jax.ShapeDtypeStruct(dense.shape, BF),
        input_output_aliases={3: 0},
        scratch_shapes=[
            pltpu.VMEM((slots, channels, BLOCK), BF),
            pltpu.VMEM((slots, channels, BLOCK), BF),
            pltpu.SemaphoreType.DMA((2, slots)),
        ],
        compiler_params=params(),
        cost_estimate=cost(64 << 30),
        name="combine_blocks",
    )(table, counts, place, dense, *backs)


def exchange(value, axis, flip):
    count = lax.axis_size(axis)
    return lax.ppermute(value, axis, [(i, i ^ flip) for i in range(count)])


def shift(value, by):
    count = lax.axis_size("dp")
    copies = count // 2
    perm = [(i, ((i // 2 + by) % copies) * 2 + i % 2) for i in range(count)]
    return lax.ppermute(value, "dp", perm)


def add(*values):
    total = values[0].astype(F32)
    for value in values[1:]:
        total = total + value.astype(F32)
    return total


def reduce_chain(keep, send):
    copies = lax.axis_size("dp") // 2
    place = lax.axis_index("dp") // 2
    half = keep.shape[0] // 2
    (got,) = yield [exchange(send, "dp", 1)]
    (crossed,) = yield [exchange(add(keep[half:], got[half:]).astype(BF), "lat", 1)]
    total = add(keep[:half], got[:half], crossed).astype(BF)
    total = total.reshape(-1, total.shape[-1])
    pieces = total.reshape(copies, -1, total.shape[-1])

    def piece(index):
        return lax.dynamic_index_in_dim(pieces, index, 0, keepdims=False)

    arrived = yield [shift(piece((place + by) % copies), by) for by in range(1, copies)]
    own = add(piece(place), *arrived).astype(BF)
    arrived = yield [shift(own, by) for by in range(1, copies)]
    whole = jnp.stack([own, *arrived])
    rows = whole.shape[1]
    if rows % 16 or keep.shape[1] % rows:
        whole = jnp.take(whole, (place - jnp.arange(copies)) % copies, axis=0)
    other, whole2 = yield [exchange(whole, "lat", 1), exchange(whole, "dp", 1)]
    (other2,) = yield [exchange(other, "dp", 1)]
    return whole, other, whole2, other2


class Rounds:
    def __init__(self):
        self.live, self.results = [], []

    def arrive(self, *others):
        sent = [values for _, values in self.live]
        sent, others = lax.optimization_barrier((sent, others))
        self.live = [(chain, values) for (chain, _), values in zip(self.live, sent)]
        return others

    def send(self):
        going = []
        for chain, values in self.live:
            try:
                going.append((chain, chain.send(values)))
            except StopIteration as stop:
                self.results.append(stop.value)
        self.live = going


def after(value, *needed):
    return lax.optimization_barrier((value, *needed))[0]


def widen_kernel(pieces, place, mine, other, mine2, other2, *refs):
    grad_in, grad_out = refs[-2:]
    core, lat, spot = place[2], place[3], place[4]
    first = core == 0
    half, channels = grad_in.shape[0] // 2, grad_in.shape[1]
    rows = half * channels // pieces
    for side, (a, b) in ((lat, (mine, mine2)), (1 - lat, (other, other2))):
        for s in range(pieces):
            start = ((spot - s + pieces) % pieces) * rows
            expert = side * half + start // channels
            here = pl.ds(pl.multiple_of(start % channels, 16), rows)
            source = pl.ds(s * rows, rows)
            grad_in[expert, here, :] = jnp.where(first, a[source], b[source]).astype(F32)
            grad_out[expert, here, :] = jnp.where(first, b[source], a[source]).astype(F32)


def widen_group(offset, size, place, whole, previous, experts, channels):
    copies, rows, hidden = whole[0].shape
    pieces = size // 2 if rows % 16 or channels % rows else copies
    args = [w.reshape(copies * rows, hidden) for w in whole]
    alias = {}
    specs = [SM] + [VM] * 4
    if previous is not None:
        alias = {5: 0, 6: 1}
        args += list(previous)
        specs += [ANY, ANY]
    block = pl.BlockSpec((size, channels, hidden), lambda i: (offset // size, 0, 0))
    return pl.pallas_call(
        functools.partial(widen_kernel, pieces),
        grid=(1,),
        in_specs=specs,
        out_specs=[block, block],
        out_shape=[jax.ShapeDtypeStruct((experts, channels, hidden), F32)] * 2,
        input_output_aliases=alias,
        compiler_params=params(),
        cost_estimate=cost(64 << 30),
        name="widen_gradients",
    )(place, *args)


def body(images, cotangent, labels, dw_kernel, ln_gain, w_expand, w_reduce, exp_in, exp_out):
    rows, channels = images.shape[1], images.shape[3]
    experts = exp_in.shape[0]
    parts = len(SIZES)
    lat = lax.axis_index("lat")
    side = lax.axis_index("exp")
    dp = lax.axis_index("dp")
    copies = lax.axis_size("dp") // 2
    place = jnp.stack([side * experts, (1 - side) * experts, dp % 2, lat, dp // 2 % copies])
    place = place.astype(jnp.int32)
    picture = jnp.swapaxes(images[0], 1, 2)
    cots = jnp.swapaxes(cotangent[0], 1, 2)
    exp_out = jnp.swapaxes(exp_out, 1, 2)
    edge = lax.dynamic_slice_in_dim(picture, jnp.where(lat == 0, rows - 3, 0), 3, axis=0)
    halo = exchange(edge, "lat", 1)
    table, counts, *cot_out = route(cots, labels.reshape(-1), place)
    theirs = exchange(counts, "exp", 1)
    cot_in = [exchange(c, "exp", 1) for c in cot_out]

    dense, *act_out = dense_part(
        picture, halo, dw_kernel, ln_gain, w_expand, w_reduce.T, place, table, counts
    )
    act_out[0] = after(act_out[0], *cot_in)
    act_in = [exchange(a, "exp", 1) for a in act_out]

    backs, grads, rounds = [], None, Rounds()
    acts = act_in[0]
    offsets = [sum(SIZES[:part]) for part in range(parts)]
    for part in range(parts):
        dense, back, keep, send = expert_part(
            offsets[part], SIZES[part], table, counts, theirs, place, dense, cots, acts,
            cot_in[part], exp_in, exp_out,
        )
        following = act_in[part + 1 : part + 2]
        if part == parts - 1:
            send, *backs = rounds.arrive(send, *backs)
        else:
            send, *following = rounds.arrive(send, *following)
        backs.append(exchange(back, "exp", 1))
        chain = reduce_chain(keep, send)
        arrived, following = lax.optimization_barrier((next(chain), following))
        rounds.live.append((chain, arrived))
        rounds.send()
        if following:
            acts = following[0]
    backs = rounds.arrive(*backs)
    rounds.send()
    output = combine(dense, backs, table, counts, place, experts)
    done = 0
    while rounds.live:
        if done:
            grads = list(rounds.arrive(*grads))
        else:
            (output,) = rounds.arrive(output)
        rounds.send()
        while done < len(rounds.results):
            grads = widen_group(
                offsets[done], SIZES[done], place, rounds.results[done], grads, experts, channels
            )
            done += 1
    output = jnp.swapaxes(output, 1, 2)[None]
    return (output, grads[0], jnp.swapaxes(grads[1], 1, 2))


def solution(mesh):
    in_specs = (
        P(("dp", "exp"), "lat", None, None),
        P(("dp", "exp"), "lat", None, None),
        P(("dp", "exp"), "lat", None, None),
        P(),
        P(),
        P(),
        P(),
        P("exp", None, None),
        P("exp", None, None),
    )
    out_specs = (P(("dp", "exp"), "lat", None, None), P("exp", None, None), P("exp", None, None))
    return jax.shard_map(body, mesh=mesh, in_specs=in_specs, out_specs=out_specs, check_vma=False)
```

```python
import functools
import jax
import jax.numpy as jnp
import numpy as np
from jax import lax
from jax.experimental import pallas as pl
from jax.experimental.pallas import tpu as pltpu
from jax.sharding import PartitionSpec as P

EXPERTS = 16
BLOCK = 128
CAP = 3
SEG = 8
TILE = 4
SIZES = (2, 2, 2, 2)
BF = jnp.bfloat16
F32 = jnp.float32
VMEM_LIMIT = 56 << 20
ANY = pl.BlockSpec(memory_space=pl.ANY)
VM = pl.BlockSpec(memory_space=pltpu.VMEM)
SM = pl.BlockSpec(memory_space=pltpu.SMEM)


def params(**more):
    return pltpu.CompilerParams(vmem_limit_bytes=VMEM_LIMIT, **more)


def cost(flops):
    return pl.CostEstimate(flops=flops, transcendentals=0, bytes_accessed=1 << 20)


def dot(a, b, dims=((1,), (0,))):
    return lax.dot_general(a, b, (dims, ((), ())), preferred_element_type=F32)


def dense_kernel(place, table, counts, images, halo, dw, gain, w1, w2, spread, gather, sums, *refs):
    dense, slots, (wide, smooth, taps, gains, w1s) = refs[0], refs[1:-5], refs[-5:]
    rows, channels, width = images.shape
    steps = width // SEG
    rest = channels - 128
    step = pl.program_id(0)
    first = step * TILE

    @pl.when(step == 0)
    def _():
        for i in range(7):
            row = dw[i]
            low, high = row[:, :128], row[:, 128:]
            for n, pair in ((0, [low, high, high]), (49, [low, low])):
                joined = jnp.concatenate(pair, axis=1)
                for j in range(7):
                    one = jnp.broadcast_to(joined[j : j + 1], (SEG, 256))
                    taps[n + 7 * i + j] = one.astype(BF)
        zero = jnp.zeros((1, rest), F32)
        low, high = gain[:, :128], gain[:, 128:]
        gains[0] = jnp.concatenate([low, high, zero], axis=1)
        gains[1] = jnp.concatenate([low, zero, high], axis=1)
        zero = jnp.zeros((rest, w1.shape[1]), BF)
        w1s[0, :128] = w1[:128]
        w1s[0, 128 : 128 + rest] = w1[128:]
        w1s[0, 128 + rest :] = zero
        w1s[1, :128] = w1[:128]
        w1s[1, 128 : 256 - rest] = zero
        w1s[1, 256 - rest :] = w1[128:]

    def picture_row(q):
        g = first - 3 + q
        inside = jnp.logical_and(g >= 0, g < rows)
        row = images[jnp.clip(g, 0, rows - 1)]
        wanted = jnp.where(place[3] == 0, g >= rows, g < 0)
        other = halo[jnp.clip(jnp.where(g < 0, g + 3, g - rows), 0, 2)]
        other = jnp.where(wanted, other, jnp.zeros_like(other))
        return jnp.where(inside, row, other)

    picture = [picture_row(q) for q in range(TILE + 6)]
    tall = []
    for q in range(TILE + 6):
        partner = picture[min(q + 2, TILE + 5)]
        joined = jnp.concatenate([picture[q], partner[128:]], axis=0)
        tall.append(dot(spread[...], joined, ((1,), (1,))))
    for q in range(TILE + 4):
        wide[q] = tall[q].astype(BF).reshape(steps + 6, SEG, 256)
    for q in range(7):
        joined = jnp.concatenate([tall[q + 2][:, :128], tall[q + 3][:, :128]], axis=1)
        wide[TILE + 4 + q] = joined.astype(BF).reshape(steps + 6, SEG, 256)

    part = 16
    parts = steps // part

    def conv(n, carry):
        unit, start = n // parts, n % parts * part
        row = jnp.where(unit == 2, TILE + 4, unit)
        kind = jnp.where(unit == 2, 49, 0)
        total = jnp.zeros((part, SEG, 256), F32)
        for i in range(7):
            source = wide[row + i, pl.ds(start, part + 6)]
            terms = [source[j : j + part] * taps[kind + 7 * i + j][None] for j in range(7)]
            low = (terms[0] + terms[1]) + (terms[2] + terms[3])
            high = (terms[4] + terms[5]) + terms[6]
            total = total + low.astype(F32) + high.astype(F32)
        rounded = total.astype(BF)
        smooth[unit, pl.ds(start, part)] = rounded
        smooth[3 + unit, pl.ds(start, part)] = (total - rounded.astype(F32)).astype(BF)
        return carry

    lax.fori_loop(0, 3 * parts, conv, 0)

    units = [smooth[u].reshape(width, 256) for u in range(6)]

    def row_of(units):
        return [
            units[0],
            units[1],
            jnp.concatenate([units[2][:, :128], units[0][:, 128:]], axis=1),
            jnp.concatenate([units[2][:, 128:], units[1][:, 128:]], axis=1),
        ]

    both, fine = row_of(units[:3]), row_of(units[3:])
    every = range(TILE)
    values = [dot(gather[...], both[h]) + dot(gather[...], fine[h]) for h in every]
    mean = [dot(values[h].astype(BF), sums[h // 2]) * (1.0 / channels) for h in every]
    c0 = [values[h][:, :128] - mean[h] for h in every]
    c1 = [values[h][:, 128:] - mean[h] for h in every]
    squares = [
        jnp.concatenate([(c0[h] * c0[h]).astype(BF), (c1[h] * c1[h]).astype(BF)], axis=1)
        for h in every
    ]
    scale = [
        lax.rsqrt(dot(squares[h], sums[h // 2]) * (1.0 / channels) + 1e-6) for h in every
    ]
    normed = [
        jnp.concatenate(
            [
                (c0[h] * scale[h] * gains[h // 2][:, :128]).astype(BF),
                (c1[h] * scale[h] * gains[h // 2][:, 128:]).astype(BF),
            ],
            axis=1,
        )
        for h in every
    ]
    active = []
    for h in every:
        expanded = dot(normed[h], w1s[h // 2])
        halved = 0.5 * expanded
        active.append((halved + halved * lax.erf(expanded * 0.7071067811865476)).astype(BF))
    for h in every:
        result = images[first + h].astype(F32) + dot(w2[...], active[h], ((1,), (1,)))
        dense[first + h] = result.astype(BF)

    @pl.when(step == pl.num_programs(0) - 1)
    def _():
        copy_slots(place, table, dense, slots)


def dense_constants(width, channels):
    steps = width // SEG
    spread = np.zeros((steps + 6, SEG, width), np.float32)
    gather = np.zeros((width, steps, SEG), np.float32)
    for s in range(SEG):
        for t in range(steps + 6):
            if 0 <= s * steps + t - 3 < width:
                spread[t, s, s * steps + t - 3] = 1
        for t in range(steps):
            gather[s * steps + t, t, s] = 1
    rest = channels - 128
    sums = np.zeros((2, 256, 128), np.float32)
    sums[:, :128] = 1
    sums[0, 128 : 128 + rest] = 1
    sums[1, 256 - rest :] = 1
    return (
        jnp.asarray(spread.reshape(-1, width), BF),
        jnp.asarray(gather.reshape(width, width), BF),
        jnp.asarray(sums, BF),
    )


def slot_shapes(channels):
    return [jax.ShapeDtypeStruct((CAP * size, channels, BLOCK), BF) for size in SIZES]


def dense_part(images, halo, dw_kernel, ln_gain, w_expand, w_reduce, place, table, counts):
    rows, channels, width = images.shape
    steps = width // SEG
    hidden = w_expand.shape[1]
    args = [images, halo, dw_kernel, ln_gain[None], w_expand, w_reduce]
    args += dense_constants(width, channels)
    slots = slot_shapes(channels)
    return pl.pallas_call(
        dense_kernel,
        grid=(rows // TILE,),
        in_specs=[SM] * 3 + [VM] * len(args),
        out_specs=[VM] * (1 + len(slots)),
        out_shape=[jax.ShapeDtypeStruct(images.shape, BF)] + slots,
        scratch_shapes=[
            pltpu.VMEM((TILE + 11, steps + 6, SEG, 256), BF),
            pltpu.VMEM((6, steps, SEG, 256), BF),
            pltpu.VMEM((98, SEG, 256), BF),
            pltpu.VMEM((2, 1, 256), F32),
            pltpu.VMEM((2, 256, hidden), BF),
        ],
        compiler_params=params(),
        cost_estimate=cost(64 << 30),
        name="dense_block",
    )(place, table, counts, *args)


def at_block(ref, b):
    return ref.at[b // 2, :, pl.ds(pl.multiple_of(b % 2 * BLOCK, BLOCK), BLOCK)]


def block_of(ref, b):
    return ref[b // 2, :, pl.ds(pl.multiple_of(b % 2 * BLOCK, BLOCK), BLOCK)]


def copy_slots(place, table, blocks, slots):
    n = CAP * place[1]
    for slot in slots:
        for k in range(slot.shape[0]):
            slot[k] = block_of(blocks, table[n + k])
        n = n + slot.shape[0]


def route_kernel(labels, place, blocks, *refs):
    table, counts, slots = refs[0], refs[1], refs[2:]
    for e in range(EXPERTS):
        counts[e] = 0
        for k in range(CAP):
            table[CAP * e + k] = 0

    def step(b, carry):
        e = labels[b]
        k = counts[e]
        table[CAP * e + k] = b
        counts[e] = k + 1
        return carry

    lax.fori_loop(0, labels.shape[0], step, 0)
    copy_slots(place, table, blocks, slots)


def route(blocks, labels, place):
    slots = slot_shapes(blocks.shape[1])
    return pl.pallas_call(
        route_kernel,
        in_specs=[SM, SM, VM],
        out_specs=[SM, SM] + [VM] * len(slots),
        out_shape=[
            jax.ShapeDtypeStruct((CAP * EXPERTS,), jnp.int32),
            jax.ShapeDtypeStruct((EXPERTS,), jnp.int32),
        ]
        + slots,
        compiler_params=params(),
        name="route_blocks",
    )(labels, place, blocks)


def expert_tokens(x, g, w_in_t, w_out_t, w_out):
    pre = dot(w_in_t, x)
    share = 0.5 + 0.5 * lax.erf(pre * 0.7071067811865476)
    hidden = (pre * share).astype(BF)
    slope = share + pre * (jnp.exp(pre * pre * -0.5) * 0.3989422804014327)
    scaled = (dot(w_out_t, g) * slope).astype(BF)
    out = dot(w_out, hidden).astype(BF)
    return out, dot(x, scaled, ((1,), (1,))), dot(g, hidden, ((1,), (1,)))


def expert_blocks(count, block, store, grads, w_in, w_out, w_in_t, w_out_t, carried):
    w_in_t[...] = w_in[...].T
    w_out_t[...] = w_out[...].T

    def load(j):
        return [jnp.where(j < count, part, jnp.zeros_like(part)) for part in block(j)]

    both = [load(0), load(1)]
    x, g = [jnp.concatenate([a, b], axis=1) for a, b in zip(*both)]
    out, grad_in, grad_out = expert_tokens(x, g, w_in_t[...], w_out_t[...], w_out[...])
    if carried is not None:
        grad_in, grad_out = grad_in + carried[0], grad_out + carried[1]
    grads[0][...] = grad_in
    grads[1][...] = grad_out
    for j in range(2):
        @pl.when(j < count)
        def _():
            store(j, x[:, j * BLOCK : (j + 1) * BLOCK], out[:, j * BLOCK : (j + 1) * BLOCK])

    @pl.when(count > 2)
    def _():
        x, g = block(2)
        out, grad_in, grad_out = expert_tokens(x, g, w_in_t[...], w_out_t[...], w_out[...])
        grads[0][...] += grad_in
        grads[1][...] += grad_out
        store(2, x, out)


def own_kernel(place, table, counts, dense_in, cots, w_in, w_out, dense, grad_in, grad_out, *scratch):
    @pl.when(pl.program_id(0) == 0)
    def _():
        dense[...] = dense_in[...]

    e = place[0] + pl.program_id(0)

    def block(j):
        b = table[CAP * e + j]
        return block_of(dense_in, b), block_of(cots, b)

    def store(j, x, out):
        b = table[CAP * e + j]
        here = pl.ds(pl.multiple_of(b % 2 * BLOCK, BLOCK), BLOCK)
        dense[b // 2, :, here] = (x.astype(F32) + out.astype(F32)).astype(BF)

    grads = (grad_in.at[0], grad_out.at[0])
    expert_blocks(counts[e], block, store, grads, w_in.at[0], w_out.at[0], *scratch, None)


def own_part(place, table, counts, dense, cots, exp_in, exp_out):
    experts, channels, hidden = exp_in.shape
    one = pl.BlockSpec((1, channels, hidden), lambda i: (i, 0, 0))
    return pl.pallas_call(
        own_kernel,
        grid=(experts,),
        in_specs=[SM, SM, SM, VM, VM, one, one],
        out_specs=[VM, one, one],
        out_shape=[jax.ShapeDtypeStruct(dense.shape, BF)]
        + [jax.ShapeDtypeStruct(exp_in.shape, F32)] * 2,
        scratch_shapes=[pltpu.VMEM((hidden, channels), BF)] * 2,
        compiler_params=params(),
        cost_estimate=cost(64 << 30),
        name="own_blocks",
    )(place, table, counts, dense, cots, exp_in, exp_out)


def far_kernel(
    offset, place, theirs, xs, gs, w_in, w_out, own_in, own_out,
    back, keep, send, w_in_t, w_out_t, grad_in, grad_out,
):
    k = pl.program_id(0)

    def block(j):
        return xs[CAP * k + j], gs[CAP * k + j]

    def store(j, x, out):
        back[CAP * k + j] = out

    count = theirs[place[0] + offset + k]
    expert_blocks(
        count, block, store, (grad_in, grad_out), w_in.at[0], w_out.at[0], w_in_t, w_out_t,
        (own_in[0], own_out[0]),
    )
    first = place[2] == 0
    a, b = grad_in[...].astype(BF), grad_out[...].astype(BF)
    keep[0] = jnp.where(first, a, b)
    send[0] = jnp.where(first, b, a)


def far_part(offset, size, place, theirs, xs, gs, exp_in, exp_out, own_in, own_out):
    channels, hidden = exp_in.shape[1:]
    one = pl.BlockSpec((1, channels, hidden), lambda i, place: (offset + i, 0, 0))
    half = size // 2
    turned = pl.BlockSpec((1, channels, hidden), lambda i, place: ((i + place[3] * half) % size, 0, 0))
    return pl.pallas_call(
        functools.partial(far_kernel, offset),
        grid_spec=pltpu.PrefetchScalarGridSpec(
            num_scalar_prefetch=1,
            grid=(size,),
            in_specs=[SM, VM, VM, one, one, one, one],
            out_specs=[VM, turned, turned],
            scratch_shapes=[pltpu.VMEM((hidden, channels), BF)] * 2
            + [pltpu.VMEM((channels, hidden), F32)] * 2,
        ),
        out_shape=[
            jax.ShapeDtypeStruct(xs.shape, BF),
            jax.ShapeDtypeStruct((size, channels, hidden), BF),
            jax.ShapeDtypeStruct((size, channels, hidden), BF),
        ],
        compiler_params=params(),
        cost_estimate=cost(64 << 30),
        name="far_blocks",
    )(place, theirs, xs, gs, exp_in, exp_out, own_in, own_out)


def combine_kernel(experts, tables, tallies, place, dense_in, *refs):
    backs, (dense, xbuf, obuf, sems) = refs[:-4], refs[-4:]
    counts = [tallies[place[1] + e] for e in range(experts)]
    table = [tables[CAP * place[1] + n] for n in range(CAP * experts)]

    def each(body):
        for slot in range(CAP * experts):
            @pl.when(slot % CAP < counts[slot // CAP])
            def _():
                body(slot)

    places = [back.at[k] for back in backs for k in range(back.shape[0])]

    def fetches(slot):
        back = places[slot]
        return (
            pltpu.make_async_copy(at_block(dense_in, table[slot]), xbuf.at[slot], sems.at[0, slot]),
            pltpu.make_async_copy(back, obuf.at[slot], sems.at[1, slot]),
        )

    def store(slot):
        return pltpu.make_async_copy(xbuf.at[slot], at_block(dense, table[slot]), sems.at[0, slot])

    def begin(slot):
        for copy in fetches(slot):
            copy.start()

    def work(slot):
        for copy in fetches(slot):
            copy.wait()
        xbuf[slot] = (xbuf[slot].astype(F32) + obuf[slot].astype(F32)).astype(BF)
        store(slot).start()

    each(begin)
    each(work)
    each(lambda slot: store(slot).wait())


def combine(dense, backs, table, counts, place, experts):
    slots = CAP * experts
    channels = dense.shape[1]
    return pl.pallas_call(
        functools.partial(combine_kernel, experts),
        in_specs=[SM] * 3 + [ANY] * (1 + len(backs)),
        out_specs=ANY,
        out_shape=jax.ShapeDtypeStruct(dense.shape, BF),
        input_output_aliases={3: 0},
        scratch_shapes=[
            pltpu.VMEM((slots, channels, BLOCK), BF),
            pltpu.VMEM((slots, channels, BLOCK), BF),
            pltpu.SemaphoreType.DMA((2, slots)),
        ],
        compiler_params=params(),
        cost_estimate=cost(64 << 30),
        name="combine_blocks",
    )(table, counts, place, dense, *backs)


def exchange(value, axis, flip):
    count = lax.axis_size(axis)
    return lax.ppermute(value, axis, [(i, i ^ flip) for i in range(count)])


def shift(value, by):
    count = lax.axis_size("dp")
    copies = count // 2
    perm = [(i, ((i // 2 + by) % copies) * 2 + i % 2) for i in range(count)]
    return lax.ppermute(value, "dp", perm)


def add(*values):
    total = values[0].astype(F32)
    for value in values[1:]:
        total = total + value.astype(F32)
    return total


CORE, LAT = -1, 0


def transfer(kind, value):
    if kind == CORE:
        return exchange(value, "dp", 1)
    if kind == LAT:
        return exchange(value, "lat", 1)
    return shift(value, kind)


def reduce_chain(keep, send):
    copies = lax.axis_size("dp") // 2
    place = lax.axis_index("dp") // 2
    half = keep.shape[0] // 2
    ways = range(1, copies)
    (got,) = yield [(CORE, send)]
    (crossed,) = yield [(LAT, add(keep[half:], got[half:]).astype(BF))]
    total = add(keep[:half], got[:half], crossed).astype(BF)
    total = total.reshape(-1, total.shape[-1])
    pieces = total.reshape(copies, -1, total.shape[-1])

    def piece(index):
        return lax.dynamic_index_in_dim(pieces, index, 0, keepdims=False)

    arrived = yield [(by, piece((place + by) % copies)) for by in ways]
    own = add(piece(place), *arrived).astype(BF)
    arrived = yield [(by, own) for by in ways]
    whole = jnp.stack([own, *arrived])
    rows = whole.shape[1]
    if rows % 16 or keep.shape[1] % rows:
        whole = jnp.take(whole, (place - jnp.arange(copies)) % copies, axis=0)
    other, whole2 = yield [(LAT, whole), (CORE, whole)]
    (other2,) = yield [(CORE, other)]
    return whole, other, whole2, other2


class Rounds:
    def __init__(self):
        self.live, self.results, self.sent = [], [], {}

    def start(self, chain):
        self.live.append((chain, next(chain)))

    def depart(self):
        ways = {}
        for _, values in self.live:
            for kind, value in values:
                ways.setdefault(kind, []).append(value.reshape(-1, value.shape[-1]))
        self.sent = {kind: transfer(kind, jnp.concatenate(flat)) for kind, flat in ways.items()}

    def arrive(self, *others):
        sent, others = lax.optimization_barrier((self.sent, others))
        live, self.live, used = self.live, [], {}
        for chain, values in live:
            got = []
            for kind, value in values:
                first = used.get(kind, 0)
                used[kind] = first + value.size // value.shape[-1]
                got.append(sent[kind][first : used[kind]].reshape(value.shape))
            try:
                self.live.append((chain, chain.send(got)))
            except StopIteration as stop:
                self.results.append(stop.value)
        self.sent = {}
        return others


def after(value, *needed):
    return lax.optimization_barrier((value, *needed))[0]


def widen_kernel(pieces, place, mine, other, mine2, other2, *refs):
    grad_in, grad_out = refs[-2:]
    core, lat, spot = place[2], place[3], place[4]
    first = core == 0
    half, channels = grad_in.shape[0] // 2, grad_in.shape[1]
    rows = half * channels // pieces
    for side, (a, b) in ((lat, (mine, mine2)), (1 - lat, (other, other2))):
        for s in range(pieces):
            start = ((spot - s + pieces) % pieces) * rows
            expert = side * half + start // channels
            here = pl.ds(pl.multiple_of(start % channels, 16), rows)
            source = pl.ds(s * rows, rows)
            grad_in[expert, here, :] = jnp.where(first, a[source], b[source]).astype(F32)
            grad_out[expert, here, :] = jnp.where(first, b[source], a[source]).astype(F32)


def widen_group(offset, size, place, whole, previous, experts, channels):
    copies, rows, hidden = whole[0].shape
    pieces = size // 2 if rows % 16 or channels % rows else copies
    args = [w.reshape(copies * rows, hidden) for w in whole]
    alias = {}
    specs = [SM] + [VM] * 4
    if previous is not None:
        alias = {5: 0, 6: 1}
        args += list(previous)
        specs += [ANY, ANY]
    block = pl.BlockSpec((size, channels, hidden), lambda i: (offset // size, 0, 0))
    return pl.pallas_call(
        functools.partial(widen_kernel, pieces),
        grid=(1,),
        in_specs=specs,
        out_specs=[block, block],
        out_shape=[jax.ShapeDtypeStruct((experts, channels, hidden), F32)] * 2,
        input_output_aliases=alias,
        compiler_params=params(),
        cost_estimate=cost(64 << 30),
        name="widen_gradients",
    )(place, *args)


def body(images, cotangent, labels, dw_kernel, ln_gain, w_expand, w_reduce, exp_in, exp_out):
    rows, channels = images.shape[1], images.shape[3]
    experts = exp_in.shape[0]
    parts = len(SIZES)
    lat = lax.axis_index("lat")
    side = lax.axis_index("exp")
    dp = lax.axis_index("dp")
    copies = lax.axis_size("dp") // 2
    place = jnp.stack([side * experts, (1 - side) * experts, dp % 2, lat, dp // 2 % copies])
    place = place.astype(jnp.int32)
    picture = jnp.swapaxes(images[0], 1, 2)
    cots = jnp.swapaxes(cotangent[0], 1, 2)
    exp_out = jnp.swapaxes(exp_out, 1, 2)
    edge = lax.dynamic_slice_in_dim(picture, jnp.where(lat == 0, rows - 3, 0), 3, axis=0)
    halo = exchange(edge, "lat", 1)
    table, counts, *cot_out = route(cots, labels.reshape(-1), place)
    theirs = exchange(counts, "exp", 1)
    cot_in = [exchange(c, "exp", 1) for c in cot_out]

    dense, *act_out = dense_part(
        picture, halo, dw_kernel, ln_gain, w_expand, w_reduce.T, place, table, counts
    )
    ahead = min(2, parts)
    act_out = [after(a, *cot_in) for a in act_out[:ahead]] + act_out[ahead:]
    act_in = [exchange(a, "exp", 1) for a in act_out[:ahead]]

    dense, *own = own_part(place, table, counts, dense, cots, exp_in, exp_out)
    act_in += [exchange(after(a, *act_in[:ahead], dense), "exp", 1) for a in act_out[ahead:]]
    backs, grads, rounds = [], None, Rounds()
    offsets = [sum(SIZES[:part]) for part in range(parts)]
    for part in range(parts):
        back, keep, send = far_part(
            offsets[part], SIZES[part], place, theirs, act_in[part], cot_in[part], exp_in, exp_out, *own
        )
        if part + 1 < parts:
            send, act_in[part + 1] = rounds.arrive(send, act_in[part + 1])
        else:
            (send,) = rounds.arrive(send)
        rounds.start(reduce_chain(keep, send))
        rounds.depart()
        backs.append(exchange(after(back, *act_in[ahead:], send), "exp", 1))
    for part in range(parts):
        (backs[part],) = rounds.arrive(backs[part])
        rounds.depart()
    output = combine(dense, backs, table, counts, place, experts)
    done = 0
    while rounds.live:
        if done:
            grads = list(rounds.arrive(*grads))
        else:
            (output,) = rounds.arrive(output)
        rounds.depart()
        while done < len(rounds.results):
            grads = widen_group(
                offsets[done], SIZES[done], place, rounds.results[done], grads, experts, channels
            )
            done += 1
    output = jnp.swapaxes(output, 1, 2)[None]
    return (output, grads[0], jnp.swapaxes(grads[1], 1, 2))


def solution(mesh):
    in_specs = (
        P(("dp", "exp"), "lat", None, None),
        P(("dp", "exp"), "lat", None, None),
        P(("dp", "exp"), "lat", None, None),
        P(),
        P(),
        P(),
        P(),
        P("exp", None, None),
        P("exp", None, None),
    )
    out_specs = (P(("dp", "exp"), "lat", None, None), P("exp", None, None), P("exp", None, None))
    return jax.shard_map(body, mesh=mesh, in_specs=in_specs, out_specs=out_specs, check_vma=False)
```

```python
import functools
import jax
import jax.numpy as jnp
import numpy as np
from jax import lax
from jax.experimental import pallas as pl
from jax.experimental.pallas import tpu as pltpu
from jax.sharding import PartitionSpec as P

EXPERTS = 16
BLOCK = 128
CAP = 3
SEG = 8
TILE = 4
SIZES = (2, 2, 2, 2)
SENT = (4, 4)
BF = jnp.bfloat16
F32 = jnp.float32
VMEM_LIMIT = 56 << 20
ANY = pl.BlockSpec(memory_space=pl.ANY)
VM = pl.BlockSpec(memory_space=pltpu.VMEM)
SM = pl.BlockSpec(memory_space=pltpu.SMEM)


def params(**more):
    return pltpu.CompilerParams(vmem_limit_bytes=VMEM_LIMIT, **more)


def cost(flops):
    return pl.CostEstimate(flops=flops, transcendentals=0, bytes_accessed=1 << 20)


def dot(a, b, dims=((1,), (0,))):
    return lax.dot_general(a, b, (dims, ((), ())), preferred_element_type=F32)


def dense_kernel(place, table, counts, images, halo, dw, gain, w1, w2, spread, gather, sums, *refs):
    dense, slots, (wide, smooth, taps, gains, w1s) = refs[0], refs[1:-5], refs[-5:]
    rows, channels, width = images.shape
    steps = width // SEG
    rest = channels - 128
    step = pl.program_id(0)
    first = step * TILE

    @pl.when(step == 0)
    def _():
        for i in range(7):
            row = dw[i]
            low, high = row[:, :128], row[:, 128:]
            for n, pair in ((0, [low, high, high]), (49, [low, low])):
                joined = jnp.concatenate(pair, axis=1)
                for j in range(7):
                    one = jnp.broadcast_to(joined[j : j + 1], (SEG, 256))
                    taps[n + 7 * i + j] = one.astype(BF)
        zero = jnp.zeros((1, rest), F32)
        low, high = gain[:, :128], gain[:, 128:]
        gains[0] = jnp.concatenate([low, high, zero], axis=1)
        gains[1] = jnp.concatenate([low, zero, high], axis=1)
        zero = jnp.zeros((rest, w1.shape[1]), BF)
        w1s[0, :128] = w1[:128]
        w1s[0, 128 : 128 + rest] = w1[128:]
        w1s[0, 128 + rest :] = zero
        w1s[1, :128] = w1[:128]
        w1s[1, 128 : 256 - rest] = zero
        w1s[1, 256 - rest :] = w1[128:]

    def picture_row(q):
        g = first - 3 + q
        inside = jnp.logical_and(g >= 0, g < rows)
        row = images[jnp.clip(g, 0, rows - 1)]
        wanted = jnp.where(place[3] == 0, g >= rows, g < 0)
        other = halo[jnp.clip(jnp.where(g < 0, g + 3, g - rows), 0, 2)]
        other = jnp.where(wanted, other, jnp.zeros_like(other))
        return jnp.where(inside, row, other)

    picture = [picture_row(q) for q in range(TILE + 6)]
    tall = []
    for q in range(TILE + 6):
        partner = picture[min(q + 2, TILE + 5)]
        joined = jnp.concatenate([picture[q], partner[128:]], axis=0)
        tall.append(dot(spread[...], joined, ((1,), (1,))))
    for q in range(TILE + 4):
        wide[q] = tall[q].astype(BF).reshape(steps + 6, SEG, 256)
    for q in range(7):
        joined = jnp.concatenate([tall[q + 2][:, :128], tall[q + 3][:, :128]], axis=1)
        wide[TILE + 4 + q] = joined.astype(BF).reshape(steps + 6, SEG, 256)

    part = 16
    parts = steps // part

    def conv(n, carry):
        unit, start = n // parts, n % parts * part
        row = jnp.where(unit == 2, TILE + 4, unit)
        kind = jnp.where(unit == 2, 49, 0)
        total = jnp.zeros((part, SEG, 256), F32)
        for i in range(7):
            source = wide[row + i, pl.ds(start, part + 6)]
            terms = [source[j : j + part] * taps[kind + 7 * i + j][None] for j in range(7)]
            low = (terms[0] + terms[1]) + (terms[2] + terms[3])
            high = (terms[4] + terms[5]) + terms[6]
            total = total + low.astype(F32) + high.astype(F32)
        rounded = total.astype(BF)
        smooth[unit, pl.ds(start, part)] = rounded
        smooth[3 + unit, pl.ds(start, part)] = (total - rounded.astype(F32)).astype(BF)
        return carry

    lax.fori_loop(0, 3 * parts, conv, 0)

    units = [smooth[u].reshape(width, 256) for u in range(6)]

    def row_of(units):
        return [
            units[0],
            units[1],
            jnp.concatenate([units[2][:, :128], units[0][:, 128:]], axis=1),
            jnp.concatenate([units[2][:, 128:], units[1][:, 128:]], axis=1),
        ]

    both, fine = row_of(units[:3]), row_of(units[3:])
    every = range(TILE)
    values = [dot(gather[...], both[h]) + dot(gather[...], fine[h]) for h in every]
    mean = [dot(values[h].astype(BF), sums[h // 2]) * (1.0 / channels) for h in every]
    c0 = [values[h][:, :128] - mean[h] for h in every]
    c1 = [values[h][:, 128:] - mean[h] for h in every]
    squares = [
        jnp.concatenate([(c0[h] * c0[h]).astype(BF), (c1[h] * c1[h]).astype(BF)], axis=1)
        for h in every
    ]
    scale = [
        lax.rsqrt(dot(squares[h], sums[h // 2]) * (1.0 / channels) + 1e-6) for h in every
    ]
    normed = [
        jnp.concatenate(
            [
                (c0[h] * scale[h] * gains[h // 2][:, :128]).astype(BF),
                (c1[h] * scale[h] * gains[h // 2][:, 128:]).astype(BF),
            ],
            axis=1,
        )
        for h in every
    ]
    active = []
    for h in every:
        expanded = dot(normed[h], w1s[h // 2])
        halved = 0.5 * expanded
        active.append((halved + halved * lax.erf(expanded * 0.7071067811865476)).astype(BF))
    for h in every:
        result = images[first + h].astype(F32) + dot(w2[...], active[h], ((1,), (1,)))
        dense[first + h] = result.astype(BF)

    @pl.when(step == pl.num_programs(0) - 1)
    def _():
        copy_slots(place, table, dense, slots)


def dense_constants(width, channels):
    steps = width // SEG
    spread = np.zeros((steps + 6, SEG, width), np.float32)
    gather = np.zeros((width, steps, SEG), np.float32)
    for s in range(SEG):
        for t in range(steps + 6):
            if 0 <= s * steps + t - 3 < width:
                spread[t, s, s * steps + t - 3] = 1
        for t in range(steps):
            gather[s * steps + t, t, s] = 1
    rest = channels - 128
    sums = np.zeros((2, 256, 128), np.float32)
    sums[:, :128] = 1
    sums[0, 128 : 128 + rest] = 1
    sums[1, 256 - rest :] = 1
    return (
        jnp.asarray(spread.reshape(-1, width), BF),
        jnp.asarray(gather.reshape(width, width), BF),
        jnp.asarray(sums, BF),
    )


def slot_shapes(channels, sizes):
    return [jax.ShapeDtypeStruct((CAP * size, channels, BLOCK), BF) for size in sizes]


def dense_part(images, halo, dw_kernel, ln_gain, w_expand, w_reduce, place, table, counts):
    rows, channels, width = images.shape
    steps = width // SEG
    hidden = w_expand.shape[1]
    args = [images, halo, dw_kernel, ln_gain[None], w_expand, w_reduce]
    args += dense_constants(width, channels)
    slots = slot_shapes(channels, SENT)
    return pl.pallas_call(
        dense_kernel,
        grid=(rows // TILE,),
        in_specs=[SM] * 3 + [VM] * len(args),
        out_specs=[VM] * (1 + len(slots)),
        out_shape=[jax.ShapeDtypeStruct(images.shape, BF)] + slots,
        scratch_shapes=[
            pltpu.VMEM((TILE + 11, steps + 6, SEG, 256), BF),
            pltpu.VMEM((6, steps, SEG, 256), BF),
            pltpu.VMEM((98, SEG, 256), BF),
            pltpu.VMEM((2, 1, 256), F32),
            pltpu.VMEM((2, 256, hidden), BF),
        ],
        compiler_params=params(),
        cost_estimate=cost(64 << 30),
        name="dense_block",
    )(place, table, counts, *args)


def at_block(ref, b):
    return ref.at[b // 2, :, pl.ds(pl.multiple_of(b % 2 * BLOCK, BLOCK), BLOCK)]


def block_of(ref, b):
    return ref[b // 2, :, pl.ds(pl.multiple_of(b % 2 * BLOCK, BLOCK), BLOCK)]


def copy_slots(place, table, blocks, slots):
    n = CAP * place[1]
    for slot in slots:
        for k in range(slot.shape[0]):
            slot[k] = block_of(blocks, table[n + k])
        n = n + slot.shape[0]


def route_kernel(labels, place, blocks, *refs):
    table, counts, slots = refs[0], refs[1], refs[2:]
    for e in range(EXPERTS):
        counts[e] = 0
        for k in range(CAP):
            table[CAP * e + k] = 0

    def step(b, carry):
        e = labels[b]
        k = counts[e]
        table[CAP * e + k] = b
        counts[e] = k + 1
        return carry

    lax.fori_loop(0, labels.shape[0], step, 0)
    copy_slots(place, table, blocks, slots)


def route(blocks, labels, place, experts):
    slots = slot_shapes(blocks.shape[1], (experts,))
    return pl.pallas_call(
        route_kernel,
        in_specs=[SM, SM, VM],
        out_specs=[SM, SM] + [VM] * len(slots),
        out_shape=[
            jax.ShapeDtypeStruct((CAP * EXPERTS,), jnp.int32),
            jax.ShapeDtypeStruct((EXPERTS,), jnp.int32),
        ]
        + slots,
        compiler_params=params(),
        name="route_blocks",
    )(labels, place, blocks)


def expert_tokens(x, g, w_in, w_out):
    pre = dot(x.T, w_in)
    share = 0.5 + 0.5 * lax.erf(pre * 0.7071067811865476)
    hidden = (pre * share).astype(BF)
    slope = share + pre * (jnp.exp(pre * pre * -0.5) * 0.3989422804014327)
    scaled = (dot(g.T, w_out) * slope).astype(BF)
    out = dot(w_out, hidden, ((1,), (1,))).astype(BF)
    return out, dot(x, scaled), dot(g, hidden)


def expert_blocks(count, block, store, grads, w_in, w_out, carried):
    def load(j):
        return [jnp.where(j < count, part, jnp.zeros_like(part)) for part in block(j)]

    both = [load(0), load(1)]
    x, g = [jnp.concatenate([a, b], axis=1) for a, b in zip(*both)]
    out, grad_in, grad_out = expert_tokens(x, g, w_in[...], w_out[...])
    if carried is not None:
        grad_in, grad_out = grad_in + carried[0], grad_out + carried[1]
    grads[0][...] = grad_in
    grads[1][...] = grad_out
    for j in range(2):
        @pl.when(j < count)
        def _():
            store(j, x[:, j * BLOCK : (j + 1) * BLOCK], out[:, j * BLOCK : (j + 1) * BLOCK])

    @pl.when(count > 2)
    def _():
        x, g = block(2)
        out, grad_in, grad_out = expert_tokens(x, g, w_in[...], w_out[...])
        grads[0][...] += grad_in
        grads[1][...] += grad_out
        store(2, x, out)


def own_kernel(place, table, counts, dense_in, cots, w_in, w_out, dense, grad_in, grad_out):
    @pl.when(pl.program_id(0) == 0)
    def _():
        dense[...] = dense_in[...]

    e = place[0] + pl.program_id(0)

    def block(j):
        b = table[CAP * e + j]
        return block_of(dense_in, b), block_of(cots, b)

    def store(j, x, out):
        b = table[CAP * e + j]
        here = pl.ds(pl.multiple_of(b % 2 * BLOCK, BLOCK), BLOCK)
        dense[b // 2, :, here] = (x.astype(F32) + out.astype(F32)).astype(BF)

    grads = (grad_in.at[0], grad_out.at[0])
    expert_blocks(counts[e], block, store, grads, w_in.at[0], w_out.at[0], None)


def own_part(place, table, counts, dense, cots, exp_in, exp_out):
    experts, channels, hidden = exp_in.shape
    one = pl.BlockSpec((1, channels, hidden), lambda i: (i, 0, 0))
    return pl.pallas_call(
        own_kernel,
        grid=(experts,),
        in_specs=[SM, SM, SM, VM, VM, one, one],
        out_specs=[VM, one, one],
        out_shape=[jax.ShapeDtypeStruct(dense.shape, BF)]
        + [jax.ShapeDtypeStruct(exp_in.shape, F32)] * 2,
        compiler_params=params(),
        cost_estimate=cost(64 << 30),
        name="own_blocks",
    )(place, table, counts, dense, cots, exp_in, exp_out)


def far_kernel(
    offset, place, theirs, xs, gs, w_in, w_out, own_in, own_out,
    back, keep, send, grad_in, grad_out,
):
    k = pl.program_id(0)

    def block(j):
        return xs[CAP * k + j], gs[CAP * k + j]

    def store(j, x, out):
        back[CAP * k + j] = out

    count = theirs[place[0] + offset + k]
    expert_blocks(
        count, block, store, (grad_in, grad_out), w_in.at[0], w_out.at[0],
        (own_in[0], own_out[0]),
    )
    first = place[2] == 0
    a, b = grad_in[...].astype(BF), grad_out[...].astype(BF)
    keep[0] = jnp.where(first, a, b)
    send[0] = jnp.where(first, b, a)


def far_part(offset, size, place, theirs, xs, gs, exp_in, exp_out, own_in, own_out):
    channels, hidden = exp_in.shape[1:]
    one = pl.BlockSpec((1, channels, hidden), lambda i, place: (offset + i, 0, 0))
    half = size // 2

    def slots(array):
        sent = array.shape[0] // CAP
        return pl.BlockSpec(
            (CAP * size, channels, BLOCK), lambda i, place: (offset % sent // size, 0, 0)
        )

    turned = pl.BlockSpec((1, channels, hidden), lambda i, place: ((i + place[3] * half) % size, 0, 0))
    return pl.pallas_call(
        functools.partial(far_kernel, offset),
        grid_spec=pltpu.PrefetchScalarGridSpec(
            num_scalar_prefetch=1,
            grid=(size,),
            in_specs=[SM, slots(xs), slots(gs), one, one, one, one],
            out_specs=[VM, turned, turned],
            scratch_shapes=[pltpu.VMEM((channels, hidden), F32)] * 2,
        ),
        out_shape=[
            jax.ShapeDtypeStruct((CAP * size, channels, BLOCK), BF),
            jax.ShapeDtypeStruct((size, channels, hidden), BF),
            jax.ShapeDtypeStruct((size, channels, hidden), BF),
        ],
        compiler_params=params(),
        cost_estimate=cost(64 << 30),
        name="far_blocks",
    )(place, theirs, xs, gs, exp_in, exp_out, own_in, own_out)


def combine_kernel(experts, tables, tallies, place, dense_in, *refs):
    backs, (dense, xbuf, obuf, sems) = refs[:-4], refs[-4:]
    counts = [tallies[place[1] + e] for e in range(experts)]
    table = [tables[CAP * place[1] + n] for n in range(CAP * experts)]

    def each(body):
        for slot in range(CAP * experts):
            @pl.when(slot % CAP < counts[slot // CAP])
            def _():
                body(slot)

    places = [back.at[k] for back in backs for k in range(back.shape[0])]

    def fetches(slot):
        back = places[slot]
        return (
            pltpu.make_async_copy(at_block(dense_in, table[slot]), xbuf.at[slot], sems.at[0, slot]),
            pltpu.make_async_copy(back, obuf.at[slot], sems.at[1, slot]),
        )

    def store(slot):
        return pltpu.make_async_copy(xbuf.at[slot], at_block(dense, table[slot]), sems.at[0, slot])

    def begin(slot):
        for copy in fetches(slot):
            copy.start()

    def work(slot):
        for copy in fetches(slot):
            copy.wait()
        xbuf[slot] = (xbuf[slot].astype(F32) + obuf[slot].astype(F32)).astype(BF)
        store(slot).start()

    each(begin)
    each(work)
    each(lambda slot: store(slot).wait())


def combine(dense, backs, table, counts, place, experts):
    slots = CAP * experts
    channels = dense.shape[1]
    return pl.pallas_call(
        functools.partial(combine_kernel, experts),
        in_specs=[SM] * 3 + [ANY] * (1 + len(backs)),
        out_specs=ANY,
        out_shape=jax.ShapeDtypeStruct(dense.shape, BF),
        input_output_aliases={3: 0},
        scratch_shapes=[
            pltpu.VMEM((slots, channels, BLOCK), BF),
            pltpu.VMEM((slots, channels, BLOCK), BF),
            pltpu.SemaphoreType.DMA((2, slots)),
        ],
        compiler_params=params(),
        cost_estimate=cost(64 << 30),
        name="combine_blocks",
    )(table, counts, place, dense, *backs)


def exchange(value, axis, flip):
    count = lax.axis_size(axis)
    return lax.ppermute(value, axis, [(i, i ^ flip) for i in range(count)])


def shift(value, by):
    count = lax.axis_size("dp")
    copies = count // 2
    perm = [(i, ((i // 2 + by) % copies) * 2 + i % 2) for i in range(count)]
    return lax.ppermute(value, "dp", perm)


def add(*values):
    total = values[0].astype(F32)
    for value in values[1:]:
        total = total + value.astype(F32)
    return total


CORE, LAT = -1, 0


def transfer(kind, value):
    if kind == CORE:
        return exchange(value, "dp", 1)
    if kind == LAT:
        return exchange(value, "lat", 1)
    return shift(value, kind)


def reduce_chain(keep, send):
    copies = lax.axis_size("dp") // 2
    place = lax.axis_index("dp") // 2
    half = keep.shape[0] // 2
    ways = range(1, copies)
    (got,) = yield [(CORE, send)]
    (crossed,) = yield [(LAT, add(keep[half:], got[half:]).astype(BF))]
    total = add(keep[:half], got[:half], crossed).astype(BF)
    total = total.reshape(-1, total.shape[-1])
    pieces = total.reshape(copies, -1, total.shape[-1])

    def piece(index):
        return lax.dynamic_index_in_dim(pieces, index, 0, keepdims=False)

    arrived = yield [(by, piece((place + by) % copies)) for by in ways]
    own = add(piece(place), *arrived).astype(BF)
    arrived = yield [(by, own) for by in ways]
    whole = jnp.stack([own, *arrived])
    rows = whole.shape[1]
    if rows % 16 or keep.shape[1] % rows:
        whole = jnp.take(whole, (place - jnp.arange(copies)) % copies, axis=0)
    other, whole2 = yield [(LAT, whole), (CORE, whole)]
    (other2,) = yield [(CORE, other)]
    return whole, other, whole2, other2


class Rounds:
    def __init__(self):
        self.live, self.results, self.sent = [], [], {}

    def start(self, chain):
        self.live.append((chain, next(chain)))

    def depart(self):
        ways = {}
        for _, values in self.live:
            for kind, value in values:
                ways.setdefault(kind, []).append(value.reshape(-1, value.shape[-1]))
        self.sent = {kind: transfer(kind, jnp.concatenate(flat)) for kind, flat in ways.items()}

    def arrive(self, *others):
        sent, others = lax.optimization_barrier((self.sent, others))
        live, self.live, used = self.live, [], {}
        for chain, values in live:
            got = []
            for kind, value in values:
                first = used.get(kind, 0)
                used[kind] = first + value.size // value.shape[-1]
                got.append(sent[kind][first : used[kind]].reshape(value.shape))
            try:
                self.live.append((chain, chain.send(got)))
            except StopIteration as stop:
                self.results.append(stop.value)
        self.sent = {}
        return others


def after(value, *needed):
    return lax.optimization_barrier((value, *needed))[0]


def widen_kernel(pieces, place, mine, other, mine2, other2, *refs):
    grad_in, grad_out = refs[-2:]
    core, lat, spot = place[2], place[3], place[4]
    first = core == 0
    half, channels = grad_in.shape[0] // 2, grad_in.shape[1]
    rows = half * channels // pieces
    for side, (a, b) in ((lat, (mine, mine2)), (1 - lat, (other, other2))):
        for s in range(pieces):
            start = ((spot - s + pieces) % pieces) * rows
            expert = side * half + start // channels
            here = pl.ds(pl.multiple_of(start % channels, 16), rows)
            source = pl.ds(s * rows, rows)
            grad_in[expert, here, :] = jnp.where(first, a[source], b[source]).astype(F32)
            grad_out[expert, here, :] = jnp.where(first, b[source], a[source]).astype(F32)


def widen_group(offset, size, place, whole, previous, experts, channels):
    copies, rows, hidden = whole[0].shape
    pieces = size // 2 if rows % 16 or channels % rows else copies
    args = [w.reshape(copies * rows, hidden) for w in whole]
    alias = {}
    specs = [SM] + [VM] * 4
    if previous is not None:
        alias = {5: 0, 6: 1}
        args += list(previous)
        specs += [ANY, ANY]
    block = pl.BlockSpec((size, channels, hidden), lambda i: (offset // size, 0, 0))
    return pl.pallas_call(
        functools.partial(widen_kernel, pieces),
        grid=(1,),
        in_specs=specs,
        out_specs=[block, block],
        out_shape=[jax.ShapeDtypeStruct((experts, channels, hidden), F32)] * 2,
        input_output_aliases=alias,
        compiler_params=params(),
        cost_estimate=cost(64 << 30),
        name="widen_gradients",
    )(place, *args)


def body(images, cotangent, labels, dw_kernel, ln_gain, w_expand, w_reduce, exp_in, exp_out):
    rows, channels = images.shape[1], images.shape[3]
    experts = exp_in.shape[0]
    parts = len(SIZES)
    lat = lax.axis_index("lat")
    side = lax.axis_index("exp")
    dp = lax.axis_index("dp")
    copies = lax.axis_size("dp") // 2
    place = jnp.stack([side * experts, (1 - side) * experts, dp % 2, lat, dp // 2 % copies])
    place = place.astype(jnp.int32)
    picture = jnp.swapaxes(images[0], 1, 2)
    cots = jnp.swapaxes(cotangent[0], 1, 2)
    exp_out = jnp.swapaxes(exp_out, 1, 2)
    edge = lax.dynamic_slice_in_dim(picture, jnp.where(lat == 0, rows - 3, 0), 3, axis=0)
    halo = exchange(edge, "lat", 1)
    table, counts, cot_out = route(cots, labels.reshape(-1), place, experts)
    theirs = exchange(counts, "exp", 1)
    cot_in = exchange(cot_out, "exp", 1)

    dense, *act_out = dense_part(
        picture, halo, dw_kernel, ln_gain, w_expand, w_reduce.T, place, table, counts
    )
    act_in = [exchange(after(act_out[0], cot_in), "exp", 1)]
    dense, *own = own_part(place, table, counts, dense, cots, exp_in, exp_out)
    for act in act_out[1:]:
        act_in.append(exchange(after(act, act_in[-1], dense), "exp", 1))
    offsets = [sum(SIZES[:part]) for part in range(parts)]
    source = [next(n for n in range(len(SENT)) if o < sum(SENT[: n + 1])) for o in offsets]
    backs, grads, rounds, done = [], None, Rounds(), 0
    for part in range(parts):
        back, keep, send = far_part(
            offsets[part], SIZES[part], place, theirs, act_in[source[part]], cot_in,
            exp_in, exp_out, *own
        )
        if part + 1 < parts and source[part + 1] != source[part]:
            coming = source[part + 1]
            send, act_in[coming] = rounds.arrive(send, act_in[coming])
        else:
            (send,) = rounds.arrive(send)
        rounds.start(reduce_chain(keep, send))
        rounds.depart()
        backs.append(exchange(after(back, act_in[-1], send), "exp", 1))
    output, turn = None, 0
    while rounds.live:
        needed = [backs[turn]] if turn < parts else [output] if turn == parts else []
        arrived = rounds.arrive(*needed, *(grads or []))
        if turn < parts:
            backs[turn] = arrived[0]
        elif turn == parts:
            output = arrived[0]
        grads = arrived[len(needed) :] or None
        rounds.depart()
        if turn == parts - 1:
            output = combine(dense, backs, table, counts, place, experts)
        turn += 1
        while done < len(rounds.results):
            grads = widen_group(
                offsets[done], SIZES[done], place, rounds.results[done], grads, experts, channels
            )
            done += 1
    output = jnp.swapaxes(output, 1, 2)[None]
    return (output, grads[0], jnp.swapaxes(grads[1], 1, 2))


def solution(mesh):
    in_specs = (
        P(("dp", "exp"), "lat", None, None),
        P(("dp", "exp"), "lat", None, None),
        P(("dp", "exp"), "lat", None, None),
        P(),
        P(),
        P(),
        P(),
        P("exp", None, None),
        P("exp", None, None),
    )
    out_specs = (P(("dp", "exp"), "lat", None, None), P("exp", None, None), P("exp", None, None))
    return jax.shard_map(body, mesh=mesh, in_specs=in_specs, out_specs=out_specs, check_vma=False)
```

```python
import functools
import jax
import jax.numpy as jnp
import numpy as np
from jax import lax
from jax.experimental import pallas as pl
from jax.experimental.pallas import tpu as pltpu
from jax.sharding import PartitionSpec as P

EXPERTS = 16
BLOCK = 128
CAP = 3
SEG = 8
TILE = 4
SIZES = (2, 2, 2, 2)
SENT = (4, 4)
BF = jnp.bfloat16
F32 = jnp.float32
VMEM_LIMIT = 56 << 20
ANY = pl.BlockSpec(memory_space=pl.ANY)
VM = pl.BlockSpec(memory_space=pltpu.VMEM)
SM = pl.BlockSpec(memory_space=pltpu.SMEM)


def params(**more):
    return pltpu.CompilerParams(vmem_limit_bytes=VMEM_LIMIT, **more)


def cost(flops):
    return pl.CostEstimate(flops=flops, transcendentals=0, bytes_accessed=1 << 20)


def dot(a, b, dims=((1,), (0,))):
    return lax.dot_general(a, b, (dims, ((), ())), preferred_element_type=F32)


def dense_kernel(place, table, counts, images, halo, dw, gain, w1, w2, spread, gather, sums, *refs):
    dense, slots, (wide, smooth, taps, gains, w1s) = refs[0], refs[1:-5], refs[-5:]
    rows, channels, width = images.shape
    steps = width // SEG
    rest = channels - 128
    step = pl.program_id(0)
    first = step * TILE

    @pl.when(step == 0)
    def _():
        for i in range(7):
            row = dw[i]
            low, high = row[:, :128], row[:, 128:]
            for n, pair in ((0, [low, high, high]), (49, [low, low])):
                joined = jnp.concatenate(pair, axis=1)
                for j in range(7):
                    one = jnp.broadcast_to(joined[j : j + 1], (SEG, 256))
                    taps[n + 7 * i + j] = one.astype(BF)
        zero = jnp.zeros((1, rest), F32)
        low, high = gain[:, :128], gain[:, 128:]
        gains[0] = jnp.concatenate([low, high, zero], axis=1)
        gains[1] = jnp.concatenate([low, zero, high], axis=1)
        zero = jnp.zeros((rest, w1.shape[1]), BF)
        w1s[0, :128] = w1[:128]
        w1s[0, 128 : 128 + rest] = w1[128:]
        w1s[0, 128 + rest :] = zero
        w1s[1, :128] = w1[:128]
        w1s[1, 128 : 256 - rest] = zero
        w1s[1, 256 - rest :] = w1[128:]

    def picture_row(q):
        g = first - 3 + q
        inside = jnp.logical_and(g >= 0, g < rows)
        row = images[jnp.clip(g, 0, rows - 1)]
        wanted = jnp.where(place[3] == 0, g >= rows, g < 0)
        other = halo[jnp.clip(jnp.where(g < 0, g + 3, g - rows), 0, 2)]
        other = jnp.where(wanted, other, jnp.zeros_like(other))
        return jnp.where(inside, row, other)

    picture = [picture_row(q) for q in range(TILE + 6)]
    tall = []
    for q in range(TILE + 6):
        partner = picture[min(q + 2, TILE + 5)]
        joined = jnp.concatenate([picture[q], partner[128:]], axis=0)
        tall.append(dot(spread[...], joined, ((1,), (1,))))
    for q in range(TILE + 4):
        wide[q] = tall[q].astype(BF).reshape(steps + 6, SEG, 256)
    for q in range(7):
        joined = jnp.concatenate([tall[q + 2][:, :128], tall[q + 3][:, :128]], axis=1)
        wide[TILE + 4 + q] = joined.astype(BF).reshape(steps + 6, SEG, 256)

    part = 32
    parts = steps // part

    def conv(n, carry):
        unit, start = n // parts, n % parts * part
        row = jnp.where(unit == 2, TILE + 4, unit)
        kind = jnp.where(unit == 2, 49, 0)
        total = jnp.zeros((part, SEG, 256), F32)
        for i in range(7):
            source = wide[row + i, pl.ds(start, part + 6)]
            terms = [source[j : j + part] * taps[kind + 7 * i + j][None] for j in range(7)]
            low = (terms[0] + terms[1]) + (terms[2] + terms[3])
            high = (terms[4] + terms[5]) + terms[6]
            total = total + low.astype(F32) + high.astype(F32)
        rounded = total.astype(BF)
        smooth[unit, pl.ds(start, part)] = rounded
        smooth[3 + unit, pl.ds(start, part)] = (total - rounded.astype(F32)).astype(BF)
        return carry

    lax.fori_loop(0, 3 * parts, conv, 0)

    units = [smooth[u].reshape(width, 256) for u in range(6)]

    def row_of(units):
        return [
            units[0],
            units[1],
            jnp.concatenate([units[2][:, :128], units[0][:, 128:]], axis=1),
            jnp.concatenate([units[2][:, 128:], units[1][:, 128:]], axis=1),
        ]

    both, fine = row_of(units[:3]), row_of(units[3:])
    every = range(TILE)
    values = [dot(gather[...], both[h]) + dot(gather[...], fine[h]) for h in every]
    mean = [dot(values[h].astype(BF), sums[h // 2]) * (1.0 / channels) for h in every]
    c0 = [values[h][:, :128] - mean[h] for h in every]
    c1 = [values[h][:, 128:] - mean[h] for h in every]
    squares = [
        jnp.concatenate([(c0[h] * c0[h]).astype(BF), (c1[h] * c1[h]).astype(BF)], axis=1)
        for h in every
    ]
    scale = [
        lax.rsqrt(dot(squares[h], sums[h // 2]) * (1.0 / channels) + 1e-6) for h in every
    ]
    normed = [
        jnp.concatenate(
            [
                (c0[h] * scale[h] * gains[h // 2][:, :128]).astype(BF),
                (c1[h] * scale[h] * gains[h // 2][:, 128:]).astype(BF),
            ],
            axis=1,
        )
        for h in every
    ]
    active = []
    for h in every:
        expanded = dot(normed[h], w1s[h // 2])
        halved = 0.5 * expanded
        active.append((halved + halved * lax.erf(expanded * 0.7071067811865476)).astype(BF))
    for h in every:
        result = images[first + h].astype(F32) + dot(w2[...], active[h], ((1,), (1,)))
        dense[first + h] = result.astype(BF)

    @pl.when(step == pl.num_programs(0) - 1)
    def _():
        copy_slots(place, table, dense, slots)


def dense_constants(width, channels):
    steps = width // SEG
    spread = np.zeros((steps + 6, SEG, width), np.float32)
    gather = np.zeros((width, steps, SEG), np.float32)
    for s in range(SEG):
        for t in range(steps + 6):
            if 0 <= s * steps + t - 3 < width:
                spread[t, s, s * steps + t - 3] = 1
        for t in range(steps):
            gather[s * steps + t, t, s] = 1
    rest = channels - 128
    sums = np.zeros((2, 256, 128), np.float32)
    sums[:, :128] = 1
    sums[0, 128 : 128 + rest] = 1
    sums[1, 256 - rest :] = 1
    return (
        jnp.asarray(spread.reshape(-1, width), BF),
        jnp.asarray(gather.reshape(width, width), BF),
        jnp.asarray(sums, BF),
    )


def slot_shapes(channels, sizes):
    return [jax.ShapeDtypeStruct((CAP * size, channels, BLOCK), BF) for size in sizes]


def dense_part(images, halo, dw_kernel, ln_gain, w_expand, w_reduce, place, table, counts):
    rows, channels, width = images.shape
    steps = width // SEG
    hidden = w_expand.shape[1]
    args = [images, halo, dw_kernel, ln_gain[None], w_expand, w_reduce]
    args += dense_constants(width, channels)
    slots = slot_shapes(channels, SENT)
    return pl.pallas_call(
        dense_kernel,
        grid=(rows // TILE,),
        in_specs=[SM] * 3 + [VM] * len(args),
        out_specs=[VM] * (1 + len(slots)),
        out_shape=[jax.ShapeDtypeStruct(images.shape, BF)] + slots,
        scratch_shapes=[
            pltpu.VMEM((TILE + 11, steps + 6, SEG, 256), BF),
            pltpu.VMEM((6, steps, SEG, 256), BF),
            pltpu.VMEM((98, SEG, 256), BF),
            pltpu.VMEM((2, 1, 256), F32),
            pltpu.VMEM((2, 256, hidden), BF),
        ],
        compiler_params=params(),
        cost_estimate=cost(64 << 30),
        name="dense_block",
    )(place, table, counts, *args)


def at_block(ref, b):
    return ref.at[b // 2, :, pl.ds(pl.multiple_of(b % 2 * BLOCK, BLOCK), BLOCK)]


def block_of(ref, b):
    return ref[b // 2, :, pl.ds(pl.multiple_of(b % 2 * BLOCK, BLOCK), BLOCK)]


def copy_slots(place, table, blocks, slots):
    n = CAP * place[1]
    for slot in slots:
        for k in range(slot.shape[0]):
            slot[k] = block_of(blocks, table[n + k])
        n = n + slot.shape[0]


def route_kernel(labels, place, blocks, *refs):
    table, counts, slots = refs[0], refs[1], refs[2:]
    for e in range(EXPERTS):
        counts[e] = 0
        for k in range(CAP):
            table[CAP * e + k] = 0

    def step(b, carry):
        e = labels[b]
        k = counts[e]
        table[CAP * e + k] = b
        counts[e] = k + 1
        return carry

    lax.fori_loop(0, labels.shape[0], step, 0)
    copy_slots(place, table, blocks, slots)


def route(blocks, labels, place, experts):
    slots = slot_shapes(blocks.shape[1], (experts,))
    return pl.pallas_call(
        route_kernel,
        in_specs=[SM, SM, VM],
        out_specs=[SM, SM] + [VM] * len(slots),
        out_shape=[
            jax.ShapeDtypeStruct((CAP * EXPERTS,), jnp.int32),
            jax.ShapeDtypeStruct((EXPERTS,), jnp.int32),
        ]
        + slots,
        compiler_params=params(),
        name="route_blocks",
    )(labels, place, blocks)


def expert_tokens(x, g, w_in, w_out):
    pre = dot(x.T, w_in)
    share = 0.5 + 0.5 * lax.erf(pre * 0.7071067811865476)
    hidden = (pre * share).astype(BF)
    slope = share + pre * (jnp.exp(pre * pre * -0.5) * 0.3989422804014327)
    scaled = (dot(g.T, w_out) * slope).astype(BF)
    out = dot(w_out, hidden, ((1,), (1,))).astype(BF)
    return out, dot(x, scaled), dot(g, hidden)


def expert_blocks(count, block, store, grads, w_in, w_out, carried):
    def load(j):
        return [jnp.where(j < count, part, jnp.zeros_like(part)) for part in block(j)]

    both = [load(0), load(1)]
    x, g = [jnp.concatenate([a, b], axis=1) for a, b in zip(*both)]
    out, grad_in, grad_out = expert_tokens(x, g, w_in[...], w_out[...])
    if carried is not None:
        grad_in, grad_out = grad_in + carried[0], grad_out + carried[1]
    grads[0][...] = grad_in
    grads[1][...] = grad_out
    for j in range(2):
        @pl.when(j < count)
        def _():
            store(j, x[:, j * BLOCK : (j + 1) * BLOCK], out[:, j * BLOCK : (j + 1) * BLOCK])

    @pl.when(count > 2)
    def _():
        x, g = block(2)
        out, grad_in, grad_out = expert_tokens(x, g, w_in[...], w_out[...])
        grads[0][...] += grad_in
        grads[1][...] += grad_out
        store(2, x, out)


def own_kernel(place, table, counts, dense_in, cots, w_in, w_out, dense, grad_in, grad_out):
    @pl.when(pl.program_id(0) == 0)
    def _():
        dense[...] = dense_in[...]

    e = place[0] + pl.program_id(0)

    def block(j):
        b = table[CAP * e + j]
        return block_of(dense_in, b), block_of(cots, b)

    def store(j, x, out):
        b = table[CAP * e + j]
        here = pl.ds(pl.multiple_of(b % 2 * BLOCK, BLOCK), BLOCK)
        dense[b // 2, :, here] = (x.astype(F32) + out.astype(F32)).astype(BF)

    grads = (grad_in.at[0], grad_out.at[0])
    expert_blocks(counts[e], block, store, grads, w_in.at[0], w_out.at[0], None)


def own_part(place, table, counts, dense, cots, exp_in, exp_out):
    experts, channels, hidden = exp_in.shape
    one = pl.BlockSpec((1, channels, hidden), lambda i: (i, 0, 0))
    return pl.pallas_call(
        own_kernel,
        grid=(experts,),
        in_specs=[SM, SM, SM, VM, VM, one, one],
        out_specs=[VM, one, one],
        out_shape=[jax.ShapeDtypeStruct(dense.shape, BF)]
        + [jax.ShapeDtypeStruct(exp_in.shape, F32)] * 2,
        compiler_params=params(),
        cost_estimate=cost(64 << 30),
        name="own_blocks",
    )(place, table, counts, dense, cots, exp_in, exp_out)


def far_kernel(
    offset, place, theirs, xs, gs, w_in, w_out, own_in, own_out,
    back, keep, send, grad_in, grad_out,
):
    k = pl.program_id(0)

    def block(j):
        return xs[CAP * k + j], gs[CAP * k + j]

    def store(j, x, out):
        back[CAP * k + j] = out

    count = theirs[place[0] + offset + k]
    expert_blocks(
        count, block, store, (grad_in, grad_out), w_in.at[0], w_out.at[0],
        (own_in[0], own_out[0]),
    )
    first = place[2] == 0
    a, b = grad_in[...].astype(BF), grad_out[...].astype(BF)
    keep[0] = jnp.where(first, a, b)
    send[0] = jnp.where(first, b, a)


def far_part(offset, size, place, theirs, xs, gs, exp_in, exp_out, own_in, own_out):
    channels, hidden = exp_in.shape[1:]
    one = pl.BlockSpec((1, channels, hidden), lambda i, place: (offset + i, 0, 0))
    half = size // 2

    def slots(array):
        sent = array.shape[0] // CAP
        return pl.BlockSpec(
            (CAP * size, channels, BLOCK), lambda i, place: (offset % sent // size, 0, 0)
        )

    turned = pl.BlockSpec((1, channels, hidden), lambda i, place: ((i + place[3] * half) % size, 0, 0))
    return pl.pallas_call(
        functools.partial(far_kernel, offset),
        grid_spec=pltpu.PrefetchScalarGridSpec(
            num_scalar_prefetch=1,
            grid=(size,),
            in_specs=[SM, slots(xs), slots(gs), one, one, one, one],
            out_specs=[VM, turned, turned],
            scratch_shapes=[pltpu.VMEM((channels, hidden), F32)] * 2,
        ),
        out_shape=[
            jax.ShapeDtypeStruct((CAP * size, channels, BLOCK), BF),
            jax.ShapeDtypeStruct((size, channels, hidden), BF),
            jax.ShapeDtypeStruct((size, channels, hidden), BF),
        ],
        compiler_params=params(),
        cost_estimate=cost(64 << 30),
        name="far_blocks",
    )(place, theirs, xs, gs, exp_in, exp_out, own_in, own_out)


def combine_kernel(experts, tables, tallies, place, dense_in, *refs):
    backs, (dense, xbuf, obuf, sems) = refs[:-4], refs[-4:]
    counts = [tallies[place[1] + e] for e in range(experts)]
    table = [tables[CAP * place[1] + n] for n in range(CAP * experts)]

    def each(body):
        for slot in range(CAP * experts):
            @pl.when(slot % CAP < counts[slot // CAP])
            def _():
                body(slot)

    places = [back.at[k] for back in backs for k in range(back.shape[0])]

    def fetches(slot):
        back = places[slot]
        return (
            pltpu.make_async_copy(at_block(dense_in, table[slot]), xbuf.at[slot], sems.at[0, slot]),
            pltpu.make_async_copy(back, obuf.at[slot], sems.at[1, slot]),
        )

    def store(slot):
        return pltpu.make_async_copy(xbuf.at[slot], at_block(dense, table[slot]), sems.at[0, slot])

    def begin(slot):
        for copy in fetches(slot):
            copy.start()

    def work(slot):
        for copy in fetches(slot):
            copy.wait()
        xbuf[slot] = (xbuf[slot].astype(F32) + obuf[slot].astype(F32)).astype(BF)
        store(slot).start()

    each(begin)
    each(work)
    each(lambda slot: store(slot).wait())


def combine(dense, backs, table, counts, place, experts):
    slots = CAP * experts
    channels = dense.shape[1]
    return pl.pallas_call(
        functools.partial(combine_kernel, experts),
        in_specs=[SM] * 3 + [ANY] * (1 + len(backs)),
        out_specs=ANY,
        out_shape=jax.ShapeDtypeStruct(dense.shape, BF),
        input_output_aliases={3: 0},
        scratch_shapes=[
            pltpu.VMEM((slots, channels, BLOCK), BF),
            pltpu.VMEM((slots, channels, BLOCK), BF),
            pltpu.SemaphoreType.DMA((2, slots)),
        ],
        compiler_params=params(),
        cost_estimate=cost(64 << 30),
        name="combine_blocks",
    )(table, counts, place, dense, *backs)


def exchange(value, axis, flip):
    count = lax.axis_size(axis)
    return lax.ppermute(value, axis, [(i, i ^ flip) for i in range(count)])


def shift(value, by):
    count = lax.axis_size("dp")
    copies = count // 2
    perm = [(i, ((i // 2 + by) % copies) * 2 + i % 2) for i in range(count)]
    return lax.ppermute(value, "dp", perm)


def add(*values):
    total = values[0].astype(F32)
    for value in values[1:]:
        total = total + value.astype(F32)
    return total


CORE, LAT = -1, 0


def transfer(kind, value):
    if kind == CORE:
        return exchange(value, "dp", 1)
    if kind == LAT:
        return exchange(value, "lat", 1)
    return shift(value, kind)


def reduce_chain(keep, send):
    copies = lax.axis_size("dp") // 2
    place = lax.axis_index("dp") // 2
    half = keep.shape[0] // 2
    ways = range(1, copies)
    (got,) = yield [(CORE, send)]
    (crossed,) = yield [(LAT, add(keep[half:], got[half:]).astype(BF))]
    total = add(keep[:half], got[:half], crossed).astype(BF)
    total = total.reshape(-1, total.shape[-1])
    pieces = total.reshape(copies, -1, total.shape[-1])

    def piece(index):
        return lax.dynamic_index_in_dim(pieces, index, 0, keepdims=False)

    arrived = yield [(by, piece((place + by) % copies)) for by in ways]
    own = add(piece(place), *arrived).astype(BF)
    arrived = yield [(by, own) for by in ways]
    whole = jnp.stack([own, *arrived])
    rows = whole.shape[1]
    if rows % 16 or keep.shape[1] % rows:
        whole = jnp.take(whole, (place - jnp.arange(copies)) % copies, axis=0)
    other, whole2 = yield [(LAT, whole), (CORE, whole)]
    (other2,) = yield [(CORE, other)]
    return whole, other, whole2, other2


class Rounds:
    def __init__(self):
        self.live, self.results, self.sent = [], [], {}

    def start(self, chain):
        self.live.append((chain, next(chain)))

    def depart(self):
        ways = {}
        for _, values in self.live:
            for kind, value in values:
                ways.setdefault(kind, []).append(value.reshape(-1, value.shape[-1]))
        self.sent = {kind: transfer(kind, jnp.concatenate(flat)) for kind, flat in sorted(ways.items(), reverse=True)}

    def arrive(self, *others):
        sent, others = lax.optimization_barrier((self.sent, others))
        live, self.live, used = self.live, [], {}
        for chain, values in live:
            got = []
            for kind, value in values:
                first = used.get(kind, 0)
                used[kind] = first + value.size // value.shape[-1]
                got.append(sent[kind][first : used[kind]].reshape(value.shape))
            try:
                self.live.append((chain, chain.send(got)))
            except StopIteration as stop:
                self.results.append(stop.value)
        self.sent = {}
        return others


def after(value, *needed):
    return lax.optimization_barrier((value, *needed))[0]


def widen_kernel(pieces, place, mine, other, mine2, other2, *refs):
    grad_in, grad_out = refs[-2:]
    core, lat, spot = place[2], place[3], place[4]
    first = core == 0
    half, channels = grad_in.shape[0] // 2, grad_in.shape[1]
    rows = half * channels // pieces
    for side, (a, b) in ((lat, (mine, mine2)), (1 - lat, (other, other2))):
        for s in range(pieces):
            start = ((spot - s + pieces) % pieces) * rows
            expert = side * half + start // channels
            here = pl.ds(pl.multiple_of(start % channels, 16), rows)
            source = pl.ds(s * rows, rows)
            grad_in[expert, here, :] = jnp.where(first, a[source], b[source]).astype(F32)
            grad_out[expert, here, :] = jnp.where(first, b[source], a[source]).astype(F32)


def widen_group(offset, size, place, whole, previous, experts, channels):
    copies, rows, hidden = whole[0].shape
    pieces = size // 2 if rows % 16 or channels % rows else copies
    args = [w.reshape(copies * rows, hidden) for w in whole]
    alias = {}
    specs = [SM] + [VM] * 4
    if previous is not None:
        alias = {5: 0, 6: 1}
        args += list(previous)
        specs += [ANY, ANY]
    block = pl.BlockSpec((size, channels, hidden), lambda i: (offset // size, 0, 0))
    return pl.pallas_call(
        functools.partial(widen_kernel, pieces),
        grid=(1,),
        in_specs=specs,
        out_specs=[block, block],
        out_shape=[jax.ShapeDtypeStruct((experts, channels, hidden), F32)] * 2,
        input_output_aliases=alias,
        compiler_params=params(),
        cost_estimate=cost(64 << 30),
        name="widen_gradients",
    )(place, *args)


def body(images, cotangent, labels, dw_kernel, ln_gain, w_expand, w_reduce, exp_in, exp_out):
    rows, channels = images.shape[1], images.shape[3]
    experts = exp_in.shape[0]
    parts = len(SIZES)
    lat = lax.axis_index("lat")
    side = lax.axis_index("exp")
    dp = lax.axis_index("dp")
    copies = lax.axis_size("dp") // 2
    place = jnp.stack([side * experts, (1 - side) * experts, dp % 2, lat, dp // 2 % copies])
    place = place.astype(jnp.int32)
    picture = jnp.swapaxes(images[0], 1, 2)
    cots = jnp.swapaxes(cotangent[0], 1, 2)
    exp_out = jnp.swapaxes(exp_out, 1, 2)
    edge = lax.dynamic_slice_in_dim(picture, jnp.where(lat == 0, rows - 3, 0), 3, axis=0)
    halo = exchange(edge, "lat", 1)
    table, counts, cot_out = route(cots, labels.reshape(-1), place, experts)
    theirs = exchange(counts, "exp", 1)
    cot_in = exchange(cot_out, "exp", 1)

    dense, *act_out = dense_part(
        picture, halo, dw_kernel, ln_gain, w_expand, w_reduce.T, place, table, counts
    )
    act_in = [exchange(after(act_out[0], cot_in), "exp", 1)]
    dense, *own = own_part(place, table, counts, dense, cots, exp_in, exp_out)
    for act in act_out[1:]:
        act_in.append(exchange(after(act, act_in[-1], dense), "exp", 1))
    offsets = [sum(SIZES[:part]) for part in range(parts)]
    source = [next(n for n in range(len(SENT)) if o < sum(SENT[: n + 1])) for o in offsets]
    backs, grads, rounds, done = [], None, Rounds(), 0
    for part in range(parts):
        back, keep, send = far_part(
            offsets[part], SIZES[part], place, theirs, act_in[source[part]], cot_in,
            exp_in, exp_out, *own
        )
        if part + 1 < parts and source[part + 1] != source[part]:
            coming = source[part + 1]
            send, act_in[coming] = rounds.arrive(send, act_in[coming])
        else:
            (send,) = rounds.arrive(send)
        rounds.start(reduce_chain(keep, send))
        rounds.depart()
        backs.append(exchange(after(back, act_in[-1], send), "exp", 1))
    output, turn = None, 0
    while rounds.live:
        needed = [backs[turn]] if turn < parts else [output] if turn == parts else []
        arrived = rounds.arrive(*needed, *(grads or []))
        if turn < parts:
            backs[turn] = arrived[0]
        elif turn == parts:
            output = arrived[0]
        grads = arrived[len(needed) :] or None
        rounds.depart()
        if turn == parts - 1:
            output = combine(dense, backs, table, counts, place, experts)
        turn += 1
        while done < len(rounds.results):
            grads = widen_group(
                offsets[done], SIZES[done], place, rounds.results[done], grads, experts, channels
            )
            done += 1
    output = jnp.swapaxes(output, 1, 2)[None]
    return (output, grads[0], jnp.swapaxes(grads[1], 1, 2))


def solution(mesh):
    in_specs = (
        P(("dp", "exp"), "lat", None, None),
        P(("dp", "exp"), "lat", None, None),
        P(("dp", "exp"), "lat", None, None),
        P(),
        P(),
        P(),
        P(),
        P("exp", None, None),
        P("exp", None, None),
    )
    out_specs = (P(("dp", "exp"), "lat", None, None), P("exp", None, None), P("exp", None, None))
    return jax.shard_map(body, mesh=mesh, in_specs=in_specs, out_specs=out_specs, check_vma=False)
```
